512 devices in a mesh: rep: 64 (over y_lo, z, core), fsdp: 8 (over y_hi, x).
Axes of the slice: x: 4, y: 4 (y_hi: 2, y_lo: 2; y = y_hi * 2 + y_lo), z: 16, core: 2. Of those that a mesh axis runs over, the one named last changes fastest.
Arguments:
- frames: bfloat16 [64, 2560, 1024], P('rep', 'fsdp'), may hold values from -6 to 6
- cotangent: bfloat16 [64, 2560, 1024], P('rep', 'fsdp'), may hold values from -0.119628906 to 0.119628906
- norm_gain: float32 [1024], replicated, may hold values from 0.25 to 1.75
- w_in: bfloat16 [1024, 2048], P('fsdp'), may hold values from -0.1875 to 0.1875
- w_out: bfloat16 [2048, 1024], P('fsdp'), may hold values from -0.1875 to 0.1875
- error_in: bfloat16 [64, 1024, 2048], P('rep', 'fsdp'), may hold values from -3 to 3
- q_start: float32 [2048, 8], replicated, may hold values from -6 to 6
- moment_one: bfloat16 [1024, 2048], P('fsdp'), may hold values from -0.035888672 to 0.035888672
- moment_two: bfloat16 [1024, 2048], P('fsdp'), may hold values from 1.9930303e-07 to 9.9658966e-05
Outputs:
- adam_step: bfloat16 [1024, 2048], P('fsdp')
- error_out: bfloat16 [64, 1024, 2048], P('rep', 'fsdp')
- q_new: float32 [2048, 8], replicated
The draws below stay inside these ranges and needn't reach their ends.
All inputs are finite; a program needn't handle non-finite values.
Results may differ from the reference program's by a relative error of at most 0.01.
Values may be sent and summed in bfloat16 or wider, within the bound.
A program may use at most 64 MiB of HBM per device.

```python
import math
import jax
import jax.numpy as jnp
from jax import lax

D = 1024
FFW = 2048
RANK = 8
TOK_DEV = 320
GROUP_TOK = 2560
N_REP = 64
N_FSDP = 8


def draw_error_in(key, part):
    key = jax.random.fold_in(key, 11)
    first, second = jax.random.split(key, 2)
    common = jax.random.normal(first, (1, D, FFW), jnp.float32)
    own = jax.random.normal(second, (N_REP, D, FFW), jnp.float32)
    values = 0.4 * common + 0.3 * own
    return jnp.clip(values, -3.0, 3.0).astype(jnp.bfloat16)


def shard_levels(own_key, shape, pieces, low, high):
    level, own = 1.0, jax.random.fold_in(own_key, 6)
    for axis_at, parts in pieces:
        draws = jnp.exp(jax.random.uniform(jax.random.fold_in(own, axis_at), (parts,), jnp.float32, low / len(pieces), high / len(pieces)))
        level = level * jnp.repeat(draws, shape[axis_at] // parts).reshape([-1 if axis == axis_at else 1 for axis in range(len(shape))])
    return level


def scatter_about(stream_key, extent, deviation, bound, cuts=(), kind=jnp.bfloat16):
    values = jax.random.normal(stream_key, extent, jnp.float32) * deviation
    if len(cuts) > 0:
        values = shard_levels(stream_key, extent, cuts, -0.22, 0.18) * values
    return jnp.clip(values, min=-bound, max=bound).astype(kind)


def setup_inputs(seed: int = 0) -> dict:
    streams_of = jax.random.split(jax.random.key(seed), 10)
    return {
        "frames": scatter_about(streams_of[0], (N_REP, GROUP_TOK, D), 1.0, 6.0, ((0, 64), (1, 8))),
        "cotangent": scatter_about(streams_of[1], (N_REP, GROUP_TOK, D), 0.02, 0.119628906, ((0, 64), (1, 8))),
        "norm_gain": jnp.clip(1.0 + 0.15 * jax.random.normal(streams_of[2], (D,), jnp.float32), 0.25, 1.75),
        "w_in": scatter_about(streams_of[3], (D, FFW), D ** -0.5, 0.1875, ((0, 8),)),
        "w_out": scatter_about(streams_of[4], (FFW, D), D ** -0.5, 0.1875, ((0, 8),)),
        "error_in": draw_error_in(jax.random.fold_in(streams_of[9], 71), 0),
        "q_start": scatter_about(streams_of[6], (FFW, RANK), 1.0, 6.0, (), jnp.float32),
        "moment_one": scatter_about(streams_of[7], (D, FFW), 0.006, 0.035888672, ((0, 8),)),
        "moment_two": jnp.clip(jnp.exp(math.log(9.965896606445312e-05) - 6.214683 * jax.random.uniform(streams_of[8], (D, FFW), jnp.float32) ** shard_levels(streams_of[8], (D, FFW), ((0, 8),), -0.2, 0.2)), 1.993030309677124e-07, 9.965896606445312e-05).astype(jnp.bfloat16),
    }


def layer_norm(values, gain):
    values = values.astype(jnp.float32)
    mean = lax.optimization_barrier(jnp.mean(values, axis=-1, keepdims=True))
    centred = values - mean
    variance = lax.optimization_barrier(jnp.mean(centred * centred, axis=-1, keepdims=True))
    return (centred * lax.rsqrt(variance + 1e-05) * gain).astype(jnp.bfloat16)

def replica_grad(frames_rep, cot_rep, norm_gain, w_in, w_out):
    normed = layer_norm(frames_rep, norm_gain).reshape(N_FSDP, TOK_DEV, D)
    cot_blocks = cot_rep.reshape(N_FSDP, TOK_DEV, D)
    hidden_pre = jnp.einsum('ftd,dk->ftk', normed.astype(jnp.float32), w_in.astype(jnp.float32))
    back_act = jnp.einsum('ftd,kd->ftk', cot_blocks.astype(jnp.float32), w_out.astype(jnp.float32))
    sig = jax.nn.sigmoid(hidden_pre)
    hidden_grad = (back_act * sig * (1.0 + hidden_pre * (1.0 - sig))).astype(jnp.bfloat16)

    def block_term(carry, pair):
        normed_block, grad_block = pair
        term = jnp.dot(normed_block.T.astype(jnp.float32), grad_block.astype(jnp.float32), preferred_element_type=jnp.float32)
        return (carry + term.astype(jnp.bfloat16).astype(jnp.float32), None)
    total, _ = lax.scan(block_term, jnp.zeros((D, FFW), jnp.float32), (normed, hidden_grad))
    return total

def reference(frames, cotangent, norm_gain, w_in, w_out, error_in, q_start, moment_one, moment_two):
    highest = lax.Precision.HIGHEST

    def one_replica(items):
        frames_rep, cot_rep, error_rep = items
        return replica_grad(frames_rep, cot_rep, norm_gain, w_in, w_out) + error_rep.astype(jnp.float32)
    compressed = lax.map(one_replica, (frames, cotangent, error_in))
    p_sum = jnp.einsum('rdk,kj->dj', compressed, q_start, precision=highest) / N_REP
    gram = jnp.dot(p_sum.T, p_sum, precision=highest)
    lower = jnp.linalg.cholesky(gram)
    p_orth = jax.scipy.linalg.solve_triangular(lower, p_sum.T, lower=True).T
    q_new = jnp.einsum('rdk,dj->kj', compressed, p_orth, precision=highest) / N_REP
    approx = jnp.dot(p_orth, q_new.T, precision=highest)
    error_out = (compressed - approx[None]).astype(jnp.bfloat16)
    m_new = 0.9 * moment_one.astype(jnp.float32) + 0.1 * approx
    v_new = 0.999 * moment_two.astype(jnp.float32) + 0.001 * approx * approx
    adam_step = m_new / (1.0 - 0.9 ** 10) / (jnp.sqrt(v_new / (1.0 - 0.999 ** 10)) + 1e-08)
    return (adam_step.astype(jnp.bfloat16), error_out, q_new)
```

```python
import functools

import jax
import jax.numpy as jnp
from jax import lax
from jax.experimental import pallas as pl
from jax.experimental.pallas import tpu as pltpu
from jax.sharding import PartitionSpec as P

MESH = pl.DeviceIdType.MESH
HIGHEST = lax.Precision.HIGHEST
F32, BF16 = jnp.float32, jnp.bfloat16

D, FFW, RANK, TOK = 1024, 2048, 8, 320
HALF = FFW // 2
BLK, BLOCKS = 256, 4
REPS = 64
SEMS = 160


def dot(left, right, left_dim, right_dim, precision=None):
    return lax.dot_general(
        left,
        right,
        (((left_dim,), (right_dim,)), ((), ())),
        precision=precision,
        preferred_element_type=F32,
    )


def kernel(
    frames, cot, gain, w_in, w_out, error, q_start, m_one, m_two,
    adam_out, error_out, q_out,
    x_buf, gain_v, norms, cots, norm_t, wi, wo, g, ra, rb, rc, mc, ty, sb, ry, rs, own, cmp,
    err_v, m1_v, m2_v, q_v, p1, p2, pt, qs, r1, q1, q2, qn, adam_v, eo_v, gram_v,
    lsem, ssem, rsem,
):
    rep, fs = lax.axis_index("rep"), lax.axis_index("fsdp")
    core, z, y_lo = lax.rem(rep, 2), lax.rem(rep // 2, 16), rep // 32
    x, y_hi = lax.rem(fs, 4), fs // 4

    def dev(y_lo=y_lo, z=z, core=core, y_hi=y_hi, x=x):
        return ((y_lo * 16 + z) * 2 + core, y_hi * 4 + x)

    x_next, x_prev, x_far = lax.rem(x + 1, 4), lax.rem(x + 3, 4), lax.rem(x + 2, 4)
    right, left = dev(x=x_next), dev(x=x_prev)
    across = dev(y_lo=1 - y_lo, y_hi=1 - y_hi)
    sibling = dev(core=1 - core)
    native = core == y_hi

    at_a = (y_lo * 2 + lax.rem(z, 2)) * 2 + core

    def peer_a(k):
        m = lax.rem(at_a + k, 8)
        return m, dev(y_lo=m // 4, z=(z // 2) * 2 + lax.rem(m // 2, 2), core=lax.rem(m, 2))

    at_b = z // 2

    def peer_b(k):
        m = lax.rem(at_b + k, 8)
        return m, dev(z=m * 2 + lax.rem(z, 2))

    at_c = fs * 2 + core

    def peer_c(k):
        m = lax.rem(at_c + k, 16)
        f = m // 2
        return m, dev(y_hi=f // 4, x=lax.rem(f, 4), core=lax.rem(m, 2))

    at_d = y_lo * 2 + lax.rem(z, 2)

    def peer_d(k):
        m = lax.rem(at_d + k, 4)
        return m, dev(y_lo=m // 2, z=(z // 2) * 2 + lax.rem(m, 2))

    ids = iter(range(SEMS))
    pending = []

    def remote(src, dst, at, device):
        return pltpu.make_async_remote_copy(
            src_ref=src, dst_ref=dst, send_sem=ssem.at[at], recv_sem=rsem.at[at],
            device_id=device, device_id_type=MESH,
        )

    def send(src, dst, at, device):
        copy = remote(src, dst, at, device)
        copy.start()
        pending.append(copy)

    def arrived(dst, at):
        remote(dst, dst, at, sibling).wait_recv()

    def in_rows(shard, start=0, count=128):
        return pl.ds(pl.multiple_of(shard * 128 + start, 64), count)

    def out_rows(shard, start=0, count=256):
        return pl.ds(pl.multiple_of(shard * 256 + start, 128), count)

    def tokens(which):
        return pl.ds(pl.multiple_of(which * TOK, TOK), TOK)

    half = w_in.at[:, pl.ds(pl.multiple_of(core * HALF, HALF), HALF)]
    f_own, f_swap = fs, y_hi * -4 + 4 + x
    local = [
        pltpu.make_async_copy(src, dst, lsem.at[at])
        for at, (src, dst) in enumerate(
            [
                (frames.at[0], x_buf),
                (gain, gain_v),
                (cot.at[0], cots.at[tokens(core)]),
                (half, wi.at[in_rows(f_own)]),
                (error.at[0], err_v),
                (q_start, q_v),
                (m_one, m1_v),
                (m_two, m2_v),
            ]
        )
    ]
    for copy in local:
        copy.start()
    own_out = pltpu.make_async_copy(w_out, wo.at[out_rows(x)], lsem.at[len(local)])

    @pl.when(native)
    def _():
        own_out.start()

    barrier = pltpu.get_barrier_semaphore()
    peers = [peer_a(k)[1] for k in range(1, 8)] + [peer_b(k)[1] for k in range(1, 8)]
    peers += [across]
    peers += [sib for f in range(1, 8) for sib in _fsdp_peers(dev, fs, f, core)]
    for peer in peers:
        pl.semaphore_signal(barrier, inc=1, device_id=peer, device_id_type=MESH)
    pl.semaphore_wait(barrier, len(peers))

    n = {name: next(ids) for name in (
        "wi_p", "wi_m", "wi_y", "ws_p", "ws_m", "wf_p", "wf_m", "wg_p", "wg_m",
        "wo_p", "wo_m", "wo_y", "of_p", "of_m", "oy_1", "oy_2", "oy_3", "oy_4", "cot", "norm",
    )}
    send(half, wi.at[in_rows(f_own)], n["wi_y"], across)
    send(half, wi.at[in_rows(f_own)], n["wi_p"], right)
    send(half, wi.at[in_rows(f_own)], n["wi_m"], left)

    def wo_send(name, shard, start, count, device, src=None):
        dst = wo.at[out_rows(shard, start, count)]
        return remote(dst if src is None else src, dst, n[name], device)

    own_sends = [
        wo_send("wo_y", x, 0, 256, across, w_out),
        wo_send("wo_p", x, 0, 256, right, w_out),
        wo_send("wo_m", x, 0, 256, left, w_out),
    ]

    @pl.when(native)
    def _():
        for copy in own_sends:
            copy.start()

    send(cot.at[0], cots.at[tokens(core)], n["cot"], sibling)

    local[0].wait()
    local[1].wait()

    @pl.loop(0, TOK // 32)
    def _(step):
        rows = pl.ds(pl.multiple_of(step * 32, 32), 32)
        values = x_buf[rows, :].astype(F32)
        centred = values - jnp.mean(values, axis=-1, keepdims=True)
        variance = jnp.mean(centred * centred, axis=-1, keepdims=True)
        result = (centred * lax.rsqrt(variance + 1e-05) * gain_v[...]).astype(BF16)
        norms[pl.ds(pl.multiple_of(core * TOK + step * 32, 32), 32), :] = result

    send(norms.at[tokens(core)], norms.at[tokens(core)], n["norm"], sibling)

    arrived(wi.at[in_rows(f_swap)], n["wi_y"])
    send(wi.at[in_rows(f_swap)], wi.at[in_rows(f_swap)], n["ws_p"], right)
    send(wi.at[in_rows(f_swap)], wi.at[in_rows(f_swap)], n["ws_m"], left)

    f_left, f_right, f_far = y_hi * 4 + x_prev, y_hi * 4 + x_next, y_hi * 4 + x_far
    g_left, g_right, g_far = [4 - y_hi * 4 + at for at in (x_prev, x_next, x_far)]

    def pass_on(shard_left, in_left, out_right, shard_right, in_right, out_left):
        arrived(wi.at[in_rows(shard_left)], n[in_left])
        first = wi.at[in_rows(shard_left, 0, 64)]
        send(first, first, n[out_right], right)
        arrived(wi.at[in_rows(shard_right)], n[in_right])
        second = wi.at[in_rows(shard_right, 64, 64)]
        send(second, second, n[out_left], left)

    pass_on(f_left, "wi_p", "wf_p", f_right, "wi_m", "wf_m")

    relays = [
        wo_send("of_p", x_prev, 0, 128, right),
        wo_send("oy_1", x_prev, 0, 256, across),
        wo_send("of_m", x_next, 128, 128, left),
        wo_send("oy_2", x_next, 0, 256, across),
        wo_send("oy_3", x_far, 0, 128, across),
        wo_send("oy_4", x_far, 128, 128, across),
    ]

    @pl.when(native)
    def _():
        arrived(wo.at[out_rows(x_prev)], n["wo_p"])
        relays[0].start()
        relays[1].start()
        arrived(wo.at[out_rows(x_next)], n["wo_m"])
        relays[2].start()
        relays[3].start()

    pass_on(g_left, "ws_p", "wg_p", g_right, "ws_m", "wg_m")

    @pl.when(native)
    def _():
        arrived(wo.at[out_rows(x_far, 0, 128)], n["of_p"])
        relays[4].start()
        arrived(wo.at[out_rows(x_far, 128, 128)], n["of_m"])
        relays[5].start()

    norm_t[core] = norms[tokens(core), :].T
    arrived(norms.at[tokens(1 - core)], n["norm"])
    norm_t[1 - core] = norms[tokens(1 - core), :].T
    arrived(cots.at[tokens(1 - core)], n["cot"])
    for copy in local[2:]:
        copy.wait()
    for shard, names in ((f_far, ("wf_p", "wf_m")), (g_far, ("wg_p", "wg_m"))):
        arrived(wi.at[in_rows(shard, 0, 64)], n[names[0]])
        arrived(wi.at[in_rows(shard, 64, 64)], n[names[1]])

    @pl.when(native)
    def _():
        own_out.wait()

    @pl.when(jnp.logical_not(native))
    def _():
        arrived(wo.at[out_rows(x)], n["wo_y"])
        arrived(wo.at[out_rows(x_prev)], n["oy_1"])
        arrived(wo.at[out_rows(x_next)], n["oy_2"])
        arrived(wo.at[out_rows(x_far, 0, 128)], n["oy_3"])
        arrived(wo.at[out_rows(x_far, 128, 128)], n["oy_4"])

    kinds = ("a_p", "a_m", "b_p", "b_m", "c_p", "c_m", "same", "cross", "sib")
    m = [{name: next(ids) for name in kinds} for _ in range(BLOCKS)]
    partner_same, partner_cross = dev(y_hi=1 - y_hi), dev(y_hi=1 - y_hi, core=1 - core)
    keep = pl.ds(pl.multiple_of(y_hi * 128, 128), 128)
    give = pl.ds(pl.multiple_of(128 - y_hi * 128, 128), 128)

    def gradient(b):
        for j in range(2):
            rows = pl.ds(j * TOK, TOK)
            pre = dot(norms[rows, :], wi[:, b * BLK : (b + 1) * BLK], 1, 0)
            act = dot(cots[rows, :], wo[b * BLK : (b + 1) * BLK, :], 1, 1)
            sig = 1.0 / (1.0 + jnp.exp(-pre))
            hidden = (act * sig * (1.0 + pre * (1.0 - sig))).astype(BF16)
            for h in range(2):
                grad = dot(norm_t[j, h * 512 : (h + 1) * 512, :], hidden, 1, 0).astype(BF16)
                for to in range(4):
                    g[b, to, j, h * 128 : (h + 1) * 128, :] = grad[to * 128 : (to + 1) * 128]
        send(g.at[b, x_far, 0], ra.at[b, 0], m[b]["a_p"], right)
        send(g.at[b, x_far, 1], ra.at[b, 1], m[b]["a_m"], left)
        send(g.at[b, x_next, 1], rb.at[b, 1], m[b]["b_p"], right)
        send(g.at[b, x_prev, 0], rb.at[b, 0], m[b]["b_m"], left)

    def merge(b):
        arrived(ra.at[b, 0], m[b]["a_p"])
        mc[b, 0] = (g[b, x_next, 0].astype(F32) + ra[b, 0].astype(F32)).astype(BF16)
        send(mc.at[b, 0], rc.at[b, 0], m[b]["c_p"], right)
        arrived(ra.at[b, 1], m[b]["a_m"])
        mc[b, 1] = (g[b, x_prev, 1].astype(F32) + ra[b, 1].astype(F32)).astype(BF16)
        send(mc.at[b, 1], rc.at[b, 1], m[b]["c_m"], left)

    def total(b, j, rows):
        return sum(ref[rows, :].astype(F32) for ref in (g.at[b, x, j], rb.at[b, j], rc.at[b, j]))

    def collect(b):
        arrived(rb.at[b, 1], m[b]["b_p"])
        arrived(rb.at[b, 0], m[b]["b_m"])
        arrived(rc.at[b, 0], m[b]["c_p"])
        arrived(rc.at[b, 1], m[b]["c_m"])
        ty[b, 0] = total(b, core, give).astype(BF16)
        send(ty.at[b, 0], ry.at[b, 0], m[b]["same"], partner_same)
        ty[b, 1] = total(b, 1 - core, give).astype(BF16)
        send(ty.at[b, 1], ry.at[b, 1], m[b]["cross"], partner_cross)
        sb[b] = total(b, 1 - core, keep).astype(BF16)
        send(sb.at[b], rs.at[b], m[b]["sib"], sibling)
        own[b] = total(b, core, keep)

    p_parts = []

    def finish(b):
        arrived(rs.at[b], m[b]["sib"])
        arrived(ry.at[b, 0], m[b]["same"])
        arrived(ry.at[b, 1], m[b]["cross"])
        for which, first, second in (
            (core, own.at[b], ry.at[b, 0]),
            (1 - core, rs.at[b], ry.at[b, 1]),
        ):
            at = which * BLOCKS + b
            columns = pl.ds(pl.multiple_of(at * BLK, BLK), BLK)
            value = first[...].astype(F32) + second[...].astype(F32) + err_v[:, columns].astype(F32)
            cmp[at] = value
            p_parts.append(dot(q_v[:, columns], value, 1, 1, HIGHEST))

    for step in range(BLOCKS + 3):
        if step < BLOCKS:
            gradient(step)
        if 0 <= step - 1 < BLOCKS:
            merge(step - 1)
        if 0 <= step - 2 < BLOCKS:
            collect(step - 2)
        if 0 <= step - 3 < BLOCKS:
            finish(step - 3)

    def exchange(buffer, at, peer, count, value):
        buffer[at] = value
        names = [next(ids) for _ in range(count - 1)]
        for k in range(1, count):
            send(buffer.at[at], buffer.at[at], names[k - 1], peer(k)[1])
        for k in range(1, count):
            arrived(buffer.at[peer(count - k)[0]], names[k - 1])
        return sum(buffer[k] for k in range(count))

    p_sum = exchange(p1, at_a, peer_a, 8, sum(p_parts))
    p_sum = exchange(p2, at_b, peer_b, 8, p_sum) * (1.0 / REPS)
    pt[...] = p_sum

    gram_v[...] = jnp.zeros_like(gram_v)
    gram_v[:, 0:RANK] = dot(p_sum, p_sum, 1, 1, HIGHEST)
    for at in range(2 * BLOCKS):
        part = dot(p_sum, cmp[at], 1, 0, HIGHEST)
        for side in range(2):
            qs[at * 2 + side, 0:8, :] = part[:, side * 128 : (side + 1) * 128]
            qs[at * 2 + side, 8:16, :] = gram_v[...]
    r1[at_c] = qs[at_c]
    names = [next(ids) for _ in range(15)]
    for k in range(1, 16):
        to, device = peer_c(k)
        send(qs.at[to], r1.at[at_c], names[k - 1], device)
    for k in range(1, 16):
        arrived(r1.at[peer_c(16 - k)[0]], names[k - 1])
    summed = sum(r1[k] for k in range(16))
    q_sum = exchange(q1, at_d, peer_d, 4, summed[0:8, :])

    gram = summed[8:16, :] * 0.5
    lane = lax.broadcasted_iota(jnp.int32, (8, 128), 1)
    row = lax.broadcasted_iota(jnp.int32, (8, 128), 0)
    inverse = jnp.where(lane == row, 1.0, 0.0).astype(F32)
    scale = jnp.zeros((8, 1), F32)
    for k in range(RANK):
        column = jnp.sum(jnp.where(lane == k, gram, 0.0), axis=1, keepdims=True)
        pivot = column[k : k + 1, :]
        scale = jnp.where(row[:, 0:1] == k, lax.rsqrt(pivot), scale)
        factor = jnp.where(row[:, 0:1] > k, column / pivot, 0.0)
        gram = gram - factor * gram[k : k + 1, :]
        inverse = inverse - factor * inverse[k : k + 1, :]
    inverse = (inverse * scale)[:, 0:RANK]
    p_orth = dot(inverse, pt[...], 1, 0, HIGHEST)

    q_sum = exchange(q2, at_b, peer_b, 8, q_sum) * (1.0 / REPS)
    qn[at_c] = dot(inverse, q_sum, 1, 0, HIGHEST)
    names = [next(ids) for _ in range(15)]
    for k in range(1, 16):
        send(qn.at[at_c], qn.at[at_c], names[k - 1], peer_c(k)[1])
    for k in range(1, 16):
        arrived(qn.at[peer_c(16 - k)[0]], names[k - 1])

    p_cols = p_orth.T
    for at in range(16):
        columns = pl.ds(at * 128, 128)
        q_v[:, columns] = qn[at]
        approx = dot(p_cols, qn[at], 1, 0, HIGHEST)
        value = cmp[at // 2, :, (at % 2) * 128 : (at % 2 + 1) * 128]
        eo_v[:, columns] = (value - approx).astype(BF16)
        m_new = 0.9 * m1_v[:, columns].astype(F32) + 0.1 * approx
        v_new = 0.999 * m2_v[:, columns].astype(F32) + 0.001 * approx * approx
        below = jnp.sqrt(v_new * (1.0 / (1.0 - 0.999**10))) + 1e-08
        adam_v[:, columns] = (m_new * (1.0 / (1.0 - 0.9**10)) / below).astype(BF16)

    last = [
        pltpu.make_async_copy(src, dst, lsem.at[at])
        for at, (src, dst) in enumerate(
            [(adam_v, adam_out), (eo_v, error_out.at[0]), (q_v, q_out)]
        )
    ]
    for copy in last:
        copy.start()
    for copy in pending:
        copy.wait_send()

    @pl.when(native)
    def _():
        for copy in own_sends + relays:
            copy.wait_send()

    for copy in last:
        copy.wait()


def _fsdp_peers(dev, fs, step, core):
    f = lax.rem(fs + step, 8)
    return [dev(y_hi=f // 4, x=lax.rem(f, 4), core=c) for c in (core, 1 - core)]


def shards(frames, cotangent, norm_gain, w_in, w_out, error_in, q_start, moment_one, moment_two):
    any_space = pl.BlockSpec(memory_space=pl.ANY)
    vmem = pltpu.VMEM
    adam, error, q_new = pl.pallas_call(
        kernel,
        out_shape=(
            jax.ShapeDtypeStruct((128, FFW), BF16),
            jax.ShapeDtypeStruct((1, 128, FFW), BF16),
            jax.ShapeDtypeStruct((RANK, FFW), F32),
        ),
        in_specs=[any_space] * 9,
        out_specs=(any_space,) * 3,
        scratch_shapes=[
            vmem((TOK, D), BF16),
            vmem((1, D), F32),
            vmem((2 * TOK, D), BF16),
            vmem((2 * TOK, D), BF16),
            vmem((2, D, TOK), BF16),
            vmem((D, HALF), BF16),
            vmem((HALF, D), BF16),
            vmem((BLOCKS, 4, 2, 256, BLK), BF16),
            vmem((BLOCKS, 2, 256, BLK), BF16),
            vmem((BLOCKS, 2, 256, BLK), BF16),
            vmem((BLOCKS, 2, 256, BLK), BF16),
            vmem((BLOCKS, 2, 256, BLK), BF16),
            vmem((BLOCKS, 2, 128, BLK), BF16),
            vmem((BLOCKS, 128, BLK), BF16),
            vmem((BLOCKS, 2, 128, BLK), BF16),
            vmem((BLOCKS, 128, BLK), BF16),
            vmem((BLOCKS, 128, BLK), F32),
            vmem((2 * BLOCKS, 128, BLK), F32),
            vmem((128, FFW), BF16),
            vmem((128, FFW), BF16),
            vmem((128, FFW), BF16),
            vmem((RANK, FFW), F32),
            vmem((8, RANK, 128), F32),
            vmem((8, RANK, 128), F32),
            vmem((RANK, 128), F32),
            vmem((16, 16, 128), F32),
            vmem((16, 16, 128), F32),
            vmem((4, RANK, 128), F32),
            vmem((8, RANK, 128), F32),
            vmem((16, RANK, 128), F32),
            vmem((128, FFW), BF16),
            vmem((128, FFW), BF16),
            vmem((RANK, 128), F32),
            pltpu.SemaphoreType.DMA((16,)),
            pltpu.SemaphoreType.DMA((SEMS,)),
            pltpu.SemaphoreType.DMA((SEMS,)),
        ],
        compiler_params=pltpu.CompilerParams(
            collective_id=0, has_side_effects=True, vmem_limit_bytes=48 * 1024 * 1024
        ),
        cost_estimate=pl.CostEstimate(
            flops=6 * TOK * D * FFW, bytes_accessed=6 << 20, transcendentals=TOK * FFW
        ),
    )(
        frames, cotangent, norm_gain.reshape(1, D), w_in, w_out, error_in, q_start.T,
        moment_one, moment_two,
    )
    return adam, error, q_new.T


def solution(mesh):
    return jax.shard_map(
        shards,
        mesh=mesh,
        in_specs=(
            P("rep", "fsdp", None),
            P("rep", "fsdp", None),
            P(),
            P("fsdp", None),
            P("fsdp", None),
            P("rep", "fsdp", None),
            P(),
            P("fsdp", None),
            P("fsdp", None),
        ),
        out_specs=(P("fsdp", None), P("rep", "fsdp", None), P()),
        check_vma=False,
    )
```

```python
import functools

import jax
import jax.numpy as jnp
from jax import lax
from jax.experimental import pallas as pl
from jax.experimental.pallas import tpu as pltpu
from jax.sharding import PartitionSpec as P

MESH = pl.DeviceIdType.MESH
HIGHEST = lax.Precision.HIGHEST
F32, BF16 = jnp.float32, jnp.bfloat16

D, FFW, RANK, TOK = 1024, 2048, 8, 320
HALF = FFW // 2
BLK, BLOCKS = 256, 4
REPS = 64
SEMS = 160


def dot(left, right, left_dim, right_dim, precision=None):
    return lax.dot_general(
        left,
        right,
        (((left_dim,), (right_dim,)), ((), ())),
        precision=precision,
        preferred_element_type=F32,
    )


def split(value):
    high = value.astype(BF16).astype(F32)
    return jnp.concatenate([high, value - high], axis=0).astype(BF16)


def halves(rows):
    return rows[0:8, :] + rows[8:16, :]


def kernel(
    frames, cot, gain, w_in, w_out, error, q_start, m_one, m_two,
    adam_out, error_out, q_out,
    x_buf, gain_v, norms, cots, norm_t, wi, wo, slope, hidden, g, ra, rb, rc, mc, ty, sb, ry, rs, own,
    err_v, m1_v, m2_v, q_v, q16, ps, p0, p1, p2, pn, qs, r1, q1, q2, qn, adam_v, eo_v, gram_v,
    known, lsem, ssem, rsem,
):
    rep, fs = lax.axis_index("rep"), lax.axis_index("fsdp")
    core, z, y_lo = lax.rem(rep, 2), lax.rem(rep // 2, 16), rep // 32
    x, y_hi = lax.rem(fs, 4), fs // 4

    def dev(y_lo=y_lo, z=z, core=core, y_hi=y_hi, x=x):
        return ((y_lo * 16 + z) * 2 + core, y_hi * 4 + x)

    x_next, x_prev, x_far = lax.rem(x + 1, 4), lax.rem(x + 3, 4), lax.rem(x + 2, 4)
    right, left = dev(x=x_next), dev(x=x_prev)
    across = dev(y_lo=1 - y_lo, y_hi=1 - y_hi)
    sibling = dev(core=1 - core)
    native = core == y_hi

    at_a = (y_lo * 2 + lax.rem(z, 2)) * 2 + core

    def peer_a(k):
        m = lax.rem(at_a + k, 8)
        return m, dev(y_lo=m // 4, z=(z // 2) * 2 + lax.rem(m // 2, 2), core=lax.rem(m, 2))

    at_b = z // 2

    def peer_b(k):
        m = lax.rem(at_b + k, 8)
        return m, dev(z=m * 2 + lax.rem(z, 2))

    at_c = fs * 2 + core

    def peer_c(k):
        m = lax.rem(at_c + k, 16)
        f = m // 2
        return m, dev(y_hi=f // 4, x=lax.rem(f, 4), core=lax.rem(m, 2))

    def peer_f(k):
        f = lax.rem(fs + k, 8)
        return f, dev(y_hi=f // 4, x=lax.rem(f, 4))

    at_d = y_lo * 2 + lax.rem(z, 2)

    def peer_d(k):
        m = lax.rem(at_d + k, 4)
        return m, dev(y_lo=m // 2, z=(z // 2) * 2 + lax.rem(m, 2))

    ids = iter(range(SEMS))
    pending = []

    def remote(src, dst, at, device):
        return pltpu.make_async_remote_copy(
            src_ref=src, dst_ref=dst, send_sem=ssem.at[at], recv_sem=rsem.at[at],
            device_id=device, device_id_type=MESH,
        )

    def send(src, dst, at, device):
        copy = remote(src, dst, at, device)
        copy.start()
        pending.append(copy)

    def arrived(dst, at):
        remote(dst, dst, at, sibling).wait_recv()

    def in_rows(shard, start=0, count=128):
        return pl.ds(pl.multiple_of(shard * 128 + start, 64), count)

    def out_rows(shard, start=0, count=256):
        return pl.ds(pl.multiple_of(shard * 256 + start, 128), count)

    def tokens(which):
        return pl.ds(pl.multiple_of(which * TOK, TOK), TOK)

    half = w_in.at[:, pl.ds(pl.multiple_of(core * HALF, HALF), HALF)]
    f_own, f_swap = fs, y_hi * -4 + 4 + x
    local = [
        pltpu.make_async_copy(src, dst, lsem.at[at])
        for at, (src, dst) in enumerate(
            [
                (frames.at[0], x_buf),
                (gain, gain_v),
                (cot.at[0], cots.at[tokens(core)]),
                (half, wi.at[in_rows(f_own)]),
                (error.at[0], err_v),
                (q_start, q_v),
                (m_one, m1_v),
                (m_two, m2_v),
            ]
        )
    ]
    for copy in local:
        copy.start()
    own_out = pltpu.make_async_copy(w_out, wo.at[out_rows(x)], lsem.at[len(local)])

    @pl.when(native)
    def _():
        own_out.start()

    barrier = pltpu.get_barrier_semaphore()
    peers = [peer_a(k)[1] for k in range(1, 8)] + [peer_b(k)[1] for k in (1, 7)]
    peers += [across]
    peers += [one for f in range(1, 8) for one in _fsdp_peers(dev, fs, f, core)]
    for peer in peers:
        pl.semaphore_signal(barrier, inc=1, device_id=peer, device_id_type=MESH)
    pl.semaphore_wait(barrier, len(peers))

    def vouch(level):
        for k in (2**level, 8 - 2**level):
            pl.semaphore_signal(
                known.at[level], inc=1, device_id=peer_b(k)[1], device_id_type=MESH
            )

    vouch(0)

    n = {name: next(ids) for name in (
        "wi_p", "wi_m", "wi_y", "ws_p", "ws_m", "wf_p", "wf_m", "wg_p", "wg_m",
        "wo_p", "wo_m", "wo_y", "of_p", "of_m", "oy_1", "oy_2", "oy_3", "oy_4", "cot", "norm",
    )}
    send(half, wi.at[in_rows(f_own)], n["wi_y"], across)
    send(half, wi.at[in_rows(f_own)], n["wi_p"], right)
    send(half, wi.at[in_rows(f_own)], n["wi_m"], left)

    def wo_send(name, shard, start, count, device, src=None):
        dst = wo.at[out_rows(shard, start, count)]
        return remote(dst if src is None else src, dst, n[name], device)

    own_sends = [
        wo_send("wo_y", x, 0, 256, across, w_out),
        wo_send("wo_p", x, 0, 256, right, w_out),
        wo_send("wo_m", x, 0, 256, left, w_out),
    ]

    @pl.when(native)
    def _():
        for copy in own_sends:
            copy.start()

    send(cot.at[0], cots.at[tokens(core)], n["cot"], sibling)

    local[0].wait()
    local[1].wait()

    @pl.loop(0, TOK // 32)
    def _(step):
        rows = pl.ds(pl.multiple_of(step * 32, 32), 32)
        values = x_buf[rows, :].astype(F32)
        centred = values - jnp.mean(values, axis=-1, keepdims=True)
        variance = jnp.mean(centred * centred, axis=-1, keepdims=True)
        result = (centred * lax.rsqrt(variance + 1e-05) * gain_v[...]).astype(BF16)
        norms[pl.ds(pl.multiple_of(core * TOK + step * 32, 32), 32), :] = result

    send(norms.at[tokens(core)], norms.at[tokens(core)], n["norm"], sibling)

    pl.semaphore_wait(known.at[0], 2)
    vouch(1)
    local[5].wait()
    q16[...] = split(q_v[...])

    arrived(wi.at[in_rows(f_swap)], n["wi_y"])
    send(wi.at[in_rows(f_swap)], wi.at[in_rows(f_swap)], n["ws_p"], right)
    send(wi.at[in_rows(f_swap)], wi.at[in_rows(f_swap)], n["ws_m"], left)

    f_left, f_right, f_far = y_hi * 4 + x_prev, y_hi * 4 + x_next, y_hi * 4 + x_far
    g_left, g_right, g_far = [4 - y_hi * 4 + at for at in (x_prev, x_next, x_far)]

    def pass_on(shard_left, in_left, out_right, shard_right, in_right, out_left):
        arrived(wi.at[in_rows(shard_left)], n[in_left])
        first = wi.at[in_rows(shard_left, 0, 64)]
        send(first, first, n[out_right], right)
        arrived(wi.at[in_rows(shard_right)], n[in_right])
        second = wi.at[in_rows(shard_right, 64, 64)]
        send(second, second, n[out_left], left)

    pass_on(f_left, "wi_p", "wf_p", f_right, "wi_m", "wf_m")

    relays = [
        wo_send("of_p", x_prev, 0, 128, right),
        wo_send("oy_1", x_prev, 0, 256, across),
        wo_send("of_m", x_next, 128, 128, left),
        wo_send("oy_2", x_next, 0, 256, across),
        wo_send("oy_3", x_far, 0, 128, across),
        wo_send("oy_4", x_far, 128, 128, across),
    ]

    @pl.when(native)
    def _():
        arrived(wo.at[out_rows(x_prev)], n["wo_p"])
        relays[0].start()
        relays[1].start()
        arrived(wo.at[out_rows(x_next)], n["wo_m"])
        relays[2].start()
        relays[3].start()

    pass_on(g_left, "ws_p", "wg_p", g_right, "ws_m", "wg_m")

    @pl.when(native)
    def _():
        arrived(wo.at[out_rows(x_far, 0, 128)], n["of_p"])
        relays[4].start()
        arrived(wo.at[out_rows(x_far, 128, 128)], n["of_m"])
        relays[5].start()

    norm_t[core] = norms[tokens(core), :].T
    arrived(norms.at[tokens(1 - core)], n["norm"])
    norm_t[1 - core] = norms[tokens(1 - core), :].T
    arrived(cots.at[tokens(1 - core)], n["cot"])
    pl.semaphore_wait(known.at[1], 2)
    for copy in local[2:5] + local[6:]:
        copy.wait()
    for shard, names in ((f_far, ("wf_p", "wf_m")), (g_far, ("wg_p", "wg_m"))):
        arrived(wi.at[in_rows(shard, 0, 64)], n[names[0]])
        arrived(wi.at[in_rows(shard, 64, 64)], n[names[1]])

    for b in range(BLOCKS):
        for j in range(2):
            rows, columns = pl.ds(j * TOK, TOK), pl.ds(b * BLK, BLK)
            pre = dot(norms[rows, :], wi[:, columns], 1, 0)
            sig = 1.0 / (1.0 + jnp.exp(-pre))
            slope[rows, columns] = sig * (1.0 + pre * (1.0 - sig))
    p_error = halves(dot(q16[...], err_v[...], 1, 1))

    @pl.when(native)
    def _():
        own_out.wait()

    @pl.when(jnp.logical_not(native))
    def _():
        arrived(wo.at[out_rows(x)], n["wo_y"])
        arrived(wo.at[out_rows(x_prev)], n["oy_1"])
        arrived(wo.at[out_rows(x_next)], n["oy_2"])
        arrived(wo.at[out_rows(x_far, 0, 128)], n["oy_3"])
        arrived(wo.at[out_rows(x_far, 128, 128)], n["oy_4"])

    u = jnp.zeros((16, 2 * TOK), F32)
    for b in range(BLOCKS):
        columns = pl.ds(b * BLK, BLK)
        act = dot(cots[...], wo[b * BLK : (b + 1) * BLK, :], 1, 1)
        hidden[:, columns] = (act * slope[:, columns]).astype(BF16)
        q_columns = pl.ds(pl.multiple_of(core * HALF + b * BLK, BLK), BLK)
        u += dot(q16[:, q_columns], hidden[:, columns], 1, 1)

    kinds = ("a_p", "a_m", "b_p", "b_m", "c_p", "c_m", "same", "cross", "sib")
    m = [{name: next(ids) for name in kinds} for _ in range(BLOCKS)]
    partner_same, partner_cross = dev(y_hi=1 - y_hi), dev(y_hi=1 - y_hi, core=1 - core)
    keep = pl.ds(pl.multiple_of(y_hi * 128, 128), 128)
    give = pl.ds(pl.multiple_of(128 - y_hi * 128, 128), 128)

    def gradient(b):
        for j in range(2):
            piece = hidden[j * TOK : (j + 1) * TOK, b * BLK : (b + 1) * BLK]
            for h in range(2):
                grad = dot(norm_t[j, h * 512 : (h + 1) * 512, :], piece, 1, 0).astype(BF16)
                for to in range(4):
                    g[b, to, j, h * 128 : (h + 1) * 128, :] = grad[to * 128 : (to + 1) * 128]
        send(g.at[b, x_far, 0], ra.at[b, 0], m[b]["a_p"], right)
        send(g.at[b, x_far, 1], ra.at[b, 1], m[b]["a_m"], left)
        send(g.at[b, x_next, 1], rb.at[b, 1], m[b]["b_p"], right)
        send(g.at[b, x_prev, 0], rb.at[b, 0], m[b]["b_m"], left)

    def merge(b):
        arrived(ra.at[b, 0], m[b]["a_p"])
        mc[b, 0] = (g[b, x_next, 0].astype(F32) + ra[b, 0].astype(F32)).astype(BF16)
        send(mc.at[b, 0], rc.at[b, 0], m[b]["c_p"], right)
        arrived(ra.at[b, 1], m[b]["a_m"])
        mc[b, 1] = (g[b, x_prev, 1].astype(F32) + ra[b, 1].astype(F32)).astype(BF16)
        send(mc.at[b, 1], rc.at[b, 1], m[b]["c_m"], left)

    def total(b, j, rows):
        return sum(ref[rows, :].astype(F32) for ref in (g.at[b, x, j], rb.at[b, j], rc.at[b, j]))

    def collect(b):
        arrived(rb.at[b, 1], m[b]["b_p"])
        arrived(rb.at[b, 0], m[b]["b_m"])
        arrived(rc.at[b, 0], m[b]["c_p"])
        arrived(rc.at[b, 1], m[b]["c_m"])
        ty[b, 0] = total(b, core, give).astype(BF16)
        send(ty.at[b, 0], ry.at[b, 0], m[b]["same"], partner_same)
        ty[b, 1] = total(b, 1 - core, give).astype(BF16)
        send(ty.at[b, 1], ry.at[b, 1], m[b]["cross"], partner_cross)
        sb[b] = total(b, 1 - core, keep).astype(BF16)
        send(sb.at[b], rs.at[b], m[b]["sib"], sibling)
        own[b] = total(b, core, keep)

    def scatter(pieces, slots, at, peer, count):
        names = [next(ids) for _ in range(count - 1)]
        for k in range(1, count):
            to, device = peer(k)
            send(pieces.at[to], slots.at[at], names[k - 1], device)
        slots[at] = pieces[at]
        return functools.partial(landed, slots, peer, count, names)

    def spread(slots, at, peer, count, value):
        slots[at] = value
        names = [next(ids) for _ in range(count - 1)]
        for k in range(1, count):
            send(slots.at[at], slots.at[at], names[k - 1], peer(k)[1])
        return functools.partial(landed, slots, peer, count, names)

    def landed(slots, peer, count, names):
        for k in range(1, count):
            arrived(slots.at[peer(count - k)[0]], names[k - 1])
        return slots

    def added(slots, count):
        return sum(slots[k] for k in range(count))

    p_part = halves(dot(split(halves(u)), norms[...], 1, 0))
    for f in range(8):
        ps[f] = p_part[:, f * 128 : (f + 1) * 128]
    done = scatter(ps, p0, fs, peer_f, 8)
    gradient(0)
    gradient(1)
    p_sum = added(done(), 8) + p_error
    p_sum = added(spread(p1, at_a, peer_a, 8, p_sum)(), 8)
    done = spread(p2, at_b, peer_b, 8, p_sum)
    merge(0)
    gradient(2)
    p_sum = added(done(), 8) * (1.0 / REPS)
    done = spread(pn, fs, peer_f, 8, p_sum)
    merge(1)
    gradient(3)
    done()
    p_all = jnp.concatenate([pn[f] for f in range(8)], axis=1)

    v = halves(dot(split(p_all), norms[...], 1, 1))
    q_hidden = halves(dot(split(v), hidden[...], 1, 0))
    q_error = halves(dot(split(p_sum), err_v[...], 1, 0))
    for at in range(16):
        qs[at] = q_error[:, at * 128 : (at + 1) * 128]
    for at in range(8):
        qs[core * 8 + at] += q_hidden[:, at * 128 : (at + 1) * 128]
    done = scatter(qs, r1, at_c, peer_c, 16)

    gram_v[...] = jnp.zeros_like(gram_v)
    gram_v[:, 0:RANK] = dot(p_all, p_all, 1, 1, HIGHEST)
    gram = gram_v[...]
    lane = lax.broadcasted_iota(jnp.int32, (8, 128), 1)
    row = lax.broadcasted_iota(jnp.int32, (8, 128), 0)
    inverse = jnp.where(lane == row, 1.0, 0.0).astype(F32)
    scale = jnp.zeros((8, 1), F32)
    for k in range(RANK):
        column = jnp.sum(jnp.where(lane == k, gram, 0.0), axis=1, keepdims=True)
        pivot = column[k : k + 1, :]
        scale = jnp.where(row[:, 0:1] == k, lax.rsqrt(pivot), scale)
        factor = jnp.where(row[:, 0:1] > k, column / pivot, 0.0)
        gram = gram - factor * gram[k : k + 1, :]
        inverse = inverse - factor * inverse[k : k + 1, :]
    inverse = (inverse * scale)[:, 0:RANK]
    p_orth = dot(inverse, p_sum, 1, 0, HIGHEST)
    high = p_orth.astype(BF16).astype(F32)
    p_cols = jnp.concatenate([high, p_orth - high, high], axis=0).T.astype(BF16)

    merge(2)
    collect(0)
    done = spread(q1, at_d, peer_d, 4, added(done(), 16))
    merge(3)
    collect(1)
    done = spread(q2, at_b, peer_b, 8, added(done(), 4))
    collect(2)
    collect(3)
    q_sum = added(done(), 8) * (1.0 / REPS)
    done = spread(qn, at_c, peer_c, 16, dot(inverse, q_sum, 1, 0, HIGHEST))
    for b in range(BLOCKS):
        arrived(rs.at[b], m[b]["sib"])
        arrived(ry.at[b, 0], m[b]["same"])
        arrived(ry.at[b, 1], m[b]["cross"])
    done()

    for which, first, second in ((core, own, 0), (1 - core, rs, 1)):
        for b in range(BLOCKS):
            for side in range(2):
                at = which * 8 + b * 2 + side
                columns = pl.ds(pl.multiple_of(at * 128, 128), 128)
                part = slice(side * 128, (side + 1) * 128)
                q_piece = qn[at]
                q_v[:, columns] = q_piece
                high = q_piece.astype(BF16).astype(F32)
                q_rows = jnp.concatenate([high, high, q_piece - high], axis=0).astype(BF16)
                approx = dot(p_cols, q_rows, 1, 0)
                value = first[b, :, part].astype(F32) + ry[b, second, :, part].astype(F32)
                value = value + err_v[:, columns].astype(F32)
                eo_v[:, columns] = (value - approx).astype(BF16)
                m_new = 0.9 * m1_v[:, columns].astype(F32) + 0.1 * approx
                v_new = 0.999 * m2_v[:, columns].astype(F32) + 0.001 * approx * approx
                below = jnp.sqrt(v_new * (1.0 / (1.0 - 0.999**10))) + 1e-08
                adam_v[:, columns] = (m_new * (1.0 / (1.0 - 0.9**10)) / below).astype(BF16)

    last = [
        pltpu.make_async_copy(src, dst, lsem.at[at])
        for at, (src, dst) in enumerate(
            [(adam_v, adam_out), (eo_v, error_out.at[0]), (q_v, q_out)]
        )
    ]
    for copy in last:
        copy.start()
    for copy in pending:
        copy.wait_send()

    @pl.when(native)
    def _():
        for copy in own_sends + relays:
            copy.wait_send()

    for copy in last:
        copy.wait()


def _fsdp_peers(dev, fs, step, core):
    f = lax.rem(fs + step, 8)
    return [dev(y_hi=f // 4, x=lax.rem(f, 4), core=c) for c in (core, 1 - core)]


def shards(frames, cotangent, norm_gain, w_in, w_out, error_in, q_start, moment_one, moment_two):
    any_space = pl.BlockSpec(memory_space=pl.ANY)
    vmem = pltpu.VMEM
    adam, error, q_new = pl.pallas_call(
        kernel,
        out_shape=(
            jax.ShapeDtypeStruct((128, FFW), BF16),
            jax.ShapeDtypeStruct((1, 128, FFW), BF16),
            jax.ShapeDtypeStruct((RANK, FFW), F32),
        ),
        in_specs=[any_space] * 9,
        out_specs=(any_space,) * 3,
        scratch_shapes=[
            vmem((TOK, D), BF16),
            vmem((1, D), F32),
            vmem((2 * TOK, D), BF16),
            vmem((2 * TOK, D), BF16),
            vmem((2, D, TOK), BF16),
            vmem((D, HALF), BF16),
            vmem((HALF, D), BF16),
            vmem((2 * TOK, HALF), F32),
            vmem((2 * TOK, HALF), BF16),
            vmem((BLOCKS, 4, 2, 256, BLK), BF16),
            vmem((BLOCKS, 2, 256, BLK), BF16),
            vmem((BLOCKS, 2, 256, BLK), BF16),
            vmem((BLOCKS, 2, 256, BLK), BF16),
            vmem((BLOCKS, 2, 256, BLK), BF16),
            vmem((BLOCKS, 2, 128, BLK), BF16),
            vmem((BLOCKS, 128, BLK), BF16),
            vmem((BLOCKS, 2, 128, BLK), BF16),
            vmem((BLOCKS, 128, BLK), BF16),
            vmem((BLOCKS, 128, BLK), F32),
            vmem((128, FFW), BF16),
            vmem((128, FFW), BF16),
            vmem((128, FFW), BF16),
            vmem((RANK, FFW), F32),
            vmem((16, FFW), BF16),
            vmem((8, RANK, 128), F32),
            vmem((8, RANK, 128), F32),
            vmem((8, RANK, 128), F32),
            vmem((8, RANK, 128), F32),
            vmem((8, RANK, 128), F32),
            vmem((16, RANK, 128), F32),
            vmem((16, RANK, 128), F32),
            vmem((4, RANK, 128), F32),
            vmem((8, RANK, 128), F32),
            vmem((16, RANK, 128), F32),
            vmem((128, FFW), BF16),
            vmem((128, FFW), BF16),
            vmem((RANK, 128), F32),
            pltpu.SemaphoreType.REGULAR((2,)),
            pltpu.SemaphoreType.DMA((16,)),
            pltpu.SemaphoreType.DMA((SEMS,)),
            pltpu.SemaphoreType.DMA((SEMS,)),
        ],
        compiler_params=pltpu.CompilerParams(
            collective_id=0, has_side_effects=True, vmem_limit_bytes=60 * 1024 * 1024
        ),
        cost_estimate=pl.CostEstimate(
            flops=6 * TOK * D * FFW, bytes_accessed=6 << 20, transcendentals=TOK * FFW
        ),
    )(
        frames, cotangent, norm_gain.reshape(1, D), w_in, w_out, error_in, q_start.T,
        moment_one, moment_two,
    )
    return adam, error, q_new.T


def solution(mesh):
    return jax.shard_map(
        shards,
        mesh=mesh,
        in_specs=(
            P("rep", "fsdp", None),
            P("rep", "fsdp", None),
            P(),
            P("fsdp", None),
            P("fsdp", None),
            P("rep", "fsdp", None),
            P(),
            P("fsdp", None),
            P("fsdp", None),
        ),
        out_specs=(P("fsdp", None), P("rep", "fsdp", None), P()),
        check_vma=False,
    )
```

```python
import functools

import jax
import jax.numpy as jnp
from jax import lax
from jax.experimental import pallas as pl
from jax.experimental.pallas import tpu as pltpu
from jax.sharding import PartitionSpec as P

MESH = pl.DeviceIdType.MESH
HIGHEST = lax.Precision.HIGHEST
F32, BF16 = jnp.float32, jnp.bfloat16

D, FFW, RANK, TOK = 1024, 2048, 8, 320
HALF = FFW // 2
BLK, BLOCKS = 256, 4
REPS = 64
SEMS = 160


def dot(left, right, left_dim, right_dim, precision=None):
    return lax.dot_general(
        left,
        right,
        (((left_dim,), (right_dim,)), ((), ())),
        precision=precision,
        preferred_element_type=F32,
    )


def split(value):
    high = value.astype(BF16).astype(F32)
    return jnp.concatenate([high, value - high], axis=0).astype(BF16)


def halves(rows):
    return rows[0:8, :] + rows[8:16, :]


def kernel(
    frames, cot, gain, w_in, w_out, error, q_start, m_one, m_two,
    adam_out, error_out, q_out,
    x_buf, gain_v, norms, cots, norm_t, wi, wo, slope, hidden, g, ra, rb, rc, mc, ty, sb, ry, rs, own,
    err_v, m1_v, m2_v, q_v, q16, ps, p0, p1, p2, pn, qs, r1, q1, q2, qn, adam_v, eo_v, gram_v,
    known, lsem, ssem, rsem,
):
    rep, fs = lax.axis_index("rep"), lax.axis_index("fsdp")
    core, z, y_lo = lax.rem(rep, 2), lax.rem(rep // 2, 16), rep // 32
    x, y_hi = lax.rem(fs, 4), fs // 4

    def dev(y_lo=y_lo, z=z, core=core, y_hi=y_hi, x=x):
        return ((y_lo * 16 + z) * 2 + core, y_hi * 4 + x)

    x_next, x_prev, x_far = lax.rem(x + 1, 4), lax.rem(x + 3, 4), lax.rem(x + 2, 4)
    right, left = dev(x=x_next), dev(x=x_prev)
    across = dev(y_lo=1 - y_lo, y_hi=1 - y_hi)
    sibling = dev(core=1 - core)
    beside, above, below = dev(y_lo=1 - y_lo), dev(z=lax.rem(z + 1, 16)), dev(z=lax.rem(z + 15, 16))
    native = core == y_hi

    at_a = (y_lo * 2 + lax.rem(z, 2)) * 2 + core

    def peer_a(k):
        m = lax.rem(at_a + k, 8)
        return m, dev(y_lo=m // 4, z=(z // 2) * 2 + lax.rem(m // 2, 2), core=lax.rem(m, 2))

    at_b = z // 2

    def peer_b(k):
        m = lax.rem(at_b + k, 8)
        return m, dev(z=m * 2 + lax.rem(z, 2))

    at_c = fs * 2 + core

    def peer_c(k):
        m = lax.rem(at_c + k, 16)
        f = m // 2
        return m, dev(y_hi=f // 4, x=lax.rem(f, 4), core=lax.rem(m, 2))

    def peer_f(k):
        f = lax.rem(fs + k, 8)
        return f, dev(y_hi=f // 4, x=lax.rem(f, 4))

    at_d = y_lo * 2 + lax.rem(z, 2)

    def peer_d(k):
        m = lax.rem(at_d + k, 4)
        return m, dev(y_lo=m // 2, z=(z // 2) * 2 + lax.rem(m, 2))

    ids = iter(range(SEMS))
    pending = []

    def remote(src, dst, at, device):
        return pltpu.make_async_remote_copy(
            src_ref=src, dst_ref=dst, send_sem=ssem.at[at], recv_sem=rsem.at[at],
            device_id=device, device_id_type=MESH,
        )

    def send(src, dst, at, device):
        copy = remote(src, dst, at, device)
        copy.start()
        pending.append(copy)

    def arrived(dst, at):
        remote(dst, dst, at, sibling).wait_recv()

    def in_rows(shard, kind, start=0, count=64):
        return wi.at[pl.ds(pl.multiple_of(shard * 128 + kind * 64 + start, 32), count)]

    def out_rows(shard, kind, start=0, count=128):
        return wo.at[pl.ds(pl.multiple_of(shard * 256 + kind * 128 + start, 64), count)]

    def tokens(which):
        return pl.ds(pl.multiple_of(which * TOK, TOK), TOK)

    half = w_in.at[:, pl.ds(pl.multiple_of(core * HALF, HALF), HALF)]
    mine = lax.rem(z + y_lo, 2)
    rest = 1 - mine

    def own_in(kind):
        return half.at[pl.ds(pl.multiple_of(kind * 64, 64), 64)]

    def own_out(kind):
        return w_out.at[pl.ds(pl.multiple_of(kind * 128, 128), 128)]

    local = [
        pltpu.make_async_copy(src, dst, lsem.at[at])
        for at, (src, dst) in enumerate(
            [
                (frames.at[0], x_buf),
                (gain, gain_v),
                (cot.at[0], cots.at[tokens(core)]),
                (half, wi.at[pl.ds(pl.multiple_of(fs * 128, 128), 128)]),
                (error.at[0], err_v),
                (q_start, q_v),
                (m_one, m1_v),
                (m_two, m2_v),
            ]
        )
    ]
    for copy in local:
        copy.start()
    base_out = pltpu.make_async_copy(
        w_out, wo.at[pl.ds(pl.multiple_of(x * 256, 256), 256)], lsem.at[len(local)]
    )

    @pl.when(native)
    def _():
        base_out.start()

    barrier = pltpu.get_barrier_semaphore()
    peers = [peer_a(k)[1] for k in range(1, 8)] + [peer_b(k)[1] for k in (1, 7)]
    peers += [across, dev(z=lax.rem(z + 15 + 2 * lax.rem(z, 2), 16))]
    peers += [one for f in range(1, 8) for one in _fsdp_peers(dev, fs, f, core)]
    for peer in peers:
        pl.semaphore_signal(barrier, inc=1, device_id=peer, device_id_type=MESH)
    pl.semaphore_wait(barrier, len(peers))

    def vouch(level):
        for k in (2**level, 8 - 2**level):
            pl.semaphore_signal(
                known.at[level], inc=1, device_id=peer_b(k)[1], device_id_type=MESH
            )

    vouch(0)

    n = {name: next(ids) for name in (
        "y1", "y2", "a_p", "a_m", "af_p", "af_m", "b_p", "b_m", "bf_p", "bf_m",
        "oy1", "oy2", "o_p", "o_m", "of_p", "of_m",
        "w1", "w2", "w3", "w4", "w5", "w6", "w7", "w8", "v1", "v2", "v3", "v4", "cot", "norm",
    )}
    g_own = 4 - y_hi * 4 + x
    f_left, f_right, f_far = y_hi * 4 + x_prev, y_hi * 4 + x_next, y_hi * 4 + x_far
    g_left, g_right, g_far = [4 - y_hi * 4 + at for at in (x_prev, x_next, x_far)]

    def pass_on(place, name, device):
        send(place, place, n[name], device)

    send(own_in(rest), in_rows(fs, rest), n["y1"], across)
    send(own_in(mine), in_rows(fs, mine), n["a_p"], right)
    send(own_in(mine), in_rows(fs, mine), n["a_m"], left)
    own_sends = [
        remote(own_out(rest), out_rows(x, rest), n["oy1"], across),
        remote(own_out(mine), out_rows(x, mine), n["o_p"], right),
        remote(own_out(mine), out_rows(x, mine), n["o_m"], left),
        remote(own_out(mine), out_rows(x, mine), n["oy2"], across),
    ]

    @pl.when(native)
    def _():
        for copy in own_sends[:3]:
            copy.start()

    send(own_in(mine), in_rows(fs, mine), n["y2"], across)

    @pl.when(native)
    def _():
        own_sends[3].start()

    send(cot.at[0], cots.at[tokens(core)], n["cot"], sibling)

    local[0].wait()
    local[1].wait()

    @pl.loop(0, TOK // 32)
    def _(step):
        rows = pl.ds(pl.multiple_of(step * 32, 32), 32)
        values = x_buf[rows, :].astype(F32)
        centred = values - jnp.mean(values, axis=-1, keepdims=True)
        variance = jnp.mean(centred * centred, axis=-1, keepdims=True)
        result = (centred * lax.rsqrt(variance + 1e-05) * gain_v[...]).astype(BF16)
        norms[pl.ds(pl.multiple_of(core * TOK + step * 32, 32), 32), :] = result

    send(norms.at[tokens(core)], norms.at[tokens(core)], n["norm"], sibling)

    local[5].wait()
    q16[...] = split(q_v[...])

    arrived(in_rows(g_own, mine), n["y1"])
    pass_on(in_rows(g_own, mine), "b_p", right)
    pass_on(in_rows(g_own, mine), "b_m", left)
    base = out_rows(x, mine)
    base_sends = [remote(base, base, n["o_p"], right), remote(base, base, n["o_m"], left)]

    @pl.when(jnp.logical_not(native))
    def _():
        arrived(base, n["oy1"])
        for copy in base_sends:
            copy.start()

    arrived(in_rows(f_left, mine), n["a_p"])
    pass_on(in_rows(f_left, mine, 0, 32), "af_p", right)
    pass_on(in_rows(f_left, mine), "w1", beside)
    arrived(in_rows(f_right, mine), n["a_m"])
    pass_on(in_rows(f_right, mine, 32, 32), "af_m", left)
    pass_on(in_rows(f_right, mine), "w2", below)

    out_sends = [
        remote(place, place, n[name], device)
        for place, name, device in (
            (out_rows(x_prev, mine, 0, 64), "of_p", right),
            (out_rows(x_prev, mine), "v1", beside),
            (out_rows(x_next, mine, 64, 64), "of_m", left),
            (out_rows(x_next, mine), "v2", below),
        )
    ]

    def pass_out():
        arrived(out_rows(x_prev, mine), n["o_p"])
        out_sends[0].start()
        out_sends[1].start()
        arrived(out_rows(x_next, mine), n["o_m"])
        out_sends[2].start()
        out_sends[3].start()

    @pl.when(native)
    def _():
        pass_out()

    pending.extend(out_sends)
    arrived(in_rows(g_left, mine), n["b_p"])
    pass_on(in_rows(g_left, mine, 0, 32), "bf_p", right)
    pass_on(in_rows(g_left, mine), "w3", above)
    arrived(in_rows(g_right, mine), n["b_m"])
    pass_on(in_rows(g_right, mine, 32, 32), "bf_m", left)
    pass_on(in_rows(g_right, mine), "w4", above)

    @pl.when(jnp.logical_not(native))
    def _():
        pass_out()

    pl.semaphore_wait(known.at[0], 2)
    vouch(1)
    for at, (name, passed, device) in enumerate((("af_p", "w5", below), ("af_m", "w6", below))):
        arrived(in_rows(f_far, mine, at * 32, 32), n[name])
        pass_on(in_rows(f_far, mine, at * 32, 32), passed, device)
    for at, (name, passed) in enumerate((("bf_p", "w7"), ("bf_m", "w8"))):
        arrived(in_rows(g_far, mine, at * 32, 32), n[name])
        pass_on(in_rows(g_far, mine, at * 32, 32), passed, beside)
    for at, (name, passed, device) in enumerate((("of_p", "v3", above), ("of_m", "v4", across))):
        arrived(out_rows(x_far, mine, at * 64, 64), n[name])
        pass_on(out_rows(x_far, mine, at * 64, 64), passed, device)

    norm_t[core] = norms[tokens(core), :].T
    arrived(norms.at[tokens(1 - core)], n["norm"])
    norm_t[1 - core] = norms[tokens(1 - core), :].T
    arrived(cots.at[tokens(1 - core)], n["cot"])
    pl.semaphore_wait(known.at[1], 2)
    for copy in local[2:5] + local[6:]:
        copy.wait()
    arrived(in_rows(g_own, rest), n["y2"])
    for shard, name in ((f_left, "w1"), (f_right, "w2"), (g_left, "w3"), (g_right, "w4")):
        arrived(in_rows(shard, rest), n[name])
    for shard, names in ((f_far, ("w5", "w6")), (g_far, ("w7", "w8"))):
        arrived(in_rows(shard, rest, 0, 32), n[names[0]])
        arrived(in_rows(shard, rest, 32, 32), n[names[1]])

    for b in range(BLOCKS):
        for j in range(2):
            rows, columns = pl.ds(j * TOK, TOK), pl.ds(b * BLK, BLK)
            pre = dot(norms[rows, :], wi[:, columns], 1, 0)
            sig = 1.0 / (1.0 + jnp.exp(-pre))
            slope[rows, columns] = sig * (1.0 + pre * (1.0 - sig))
    p_error = halves(dot(q16[...], err_v[...], 1, 1))

    @pl.when(native)
    def _():
        base_out.wait()

    @pl.when(jnp.logical_not(native))
    def _():
        arrived(out_rows(x, rest), n["oy2"])

    arrived(out_rows(x_prev, rest), n["v1"])
    arrived(out_rows(x_next, rest), n["v2"])
    arrived(out_rows(x_far, rest, 0, 64), n["v3"])
    arrived(out_rows(x_far, rest, 64, 64), n["v4"])

    u = jnp.zeros((16, 2 * TOK), F32)
    for b in range(BLOCKS):
        columns = pl.ds(b * BLK, BLK)
        act = dot(cots[...], wo[b * BLK : (b + 1) * BLK, :], 1, 1)
        hidden[:, columns] = (act * slope[:, columns]).astype(BF16)
        q_columns = pl.ds(pl.multiple_of(core * HALF + b * BLK, BLK), BLK)
        u += dot(q16[:, q_columns], hidden[:, columns], 1, 1)

    kinds = ("a_p", "a_m", "b_p", "b_m", "c_p", "c_m", "same", "cross", "sib")
    m = [{name: next(ids) for name in kinds} for _ in range(BLOCKS)]
    partner_same, partner_cross = dev(y_hi=1 - y_hi), dev(y_hi=1 - y_hi, core=1 - core)
    keep = pl.ds(pl.multiple_of(y_hi * 128, 128), 128)
    give = pl.ds(pl.multiple_of(128 - y_hi * 128, 128), 128)

    def gradient(b):
        for j in range(2):
            piece = hidden[j * TOK : (j + 1) * TOK, b * BLK : (b + 1) * BLK]
            for h in range(2):
                grad = dot(norm_t[j, h * 512 : (h + 1) * 512, :], piece, 1, 0).astype(BF16)
                for to in range(4):
                    g[b, to, j, h * 128 : (h + 1) * 128, :] = grad[to * 128 : (to + 1) * 128]

    def depart(b):
        send(g.at[b, x_far, 0], ra.at[b, 0], m[b]["a_p"], right)
        send(g.at[b, x_far, 1], ra.at[b, 1], m[b]["a_m"], left)
        send(g.at[b, x_next, 1], rb.at[b, 1], m[b]["b_p"], right)
        send(g.at[b, x_prev, 0], rb.at[b, 0], m[b]["b_m"], left)

    def merge(b):
        arrived(ra.at[b, 0], m[b]["a_p"])
        mc[b, 0] = (g[b, x_next, 0].astype(F32) + ra[b, 0].astype(F32)).astype(BF16)
        send(mc.at[b, 0], rc.at[b, 0], m[b]["c_p"], right)
        arrived(ra.at[b, 1], m[b]["a_m"])
        mc[b, 1] = (g[b, x_prev, 1].astype(F32) + ra[b, 1].astype(F32)).astype(BF16)
        send(mc.at[b, 1], rc.at[b, 1], m[b]["c_m"], left)

    def total(b, j, rows):
        return sum(ref[rows, :].astype(F32) for ref in (g.at[b, x, j], rb.at[b, j], rc.at[b, j]))

    def collect(b):
        arrived(rb.at[b, 1], m[b]["b_p"])
        arrived(rb.at[b, 0], m[b]["b_m"])
        arrived(rc.at[b, 0], m[b]["c_p"])
        arrived(rc.at[b, 1], m[b]["c_m"])
        ty[b, 0] = total(b, core, give).astype(BF16)
        send(ty.at[b, 0], ry.at[b, 0], m[b]["same"], partner_same)
        ty[b, 1] = total(b, 1 - core, give).astype(BF16)
        send(ty.at[b, 1], ry.at[b, 1], m[b]["cross"], partner_cross)
        sb[b] = total(b, 1 - core, keep).astype(BF16)
        send(sb.at[b], rs.at[b], m[b]["sib"], sibling)
        own[b] = total(b, core, keep)

    def scatter(pieces, slots, at, peer, count):
        names = [next(ids) for _ in range(count - 1)]
        for k in range(1, count):
            to, device = peer(k)
            send(pieces.at[to], slots.at[at], names[k - 1], device)
        slots[at] = pieces[at]
        return functools.partial(landed, slots, peer, count, names)

    def spread(slots, at, peer, count, value):
        slots[at] = value
        names = [next(ids) for _ in range(count - 1)]
        for k in range(1, count):
            send(slots.at[at], slots.at[at], names[k - 1], peer(k)[1])
        return functools.partial(landed, slots, peer, count, names)

    def landed(slots, peer, count, names):
        for k in range(1, count):
            arrived(slots.at[peer(count - k)[0]], names[k - 1])
        return slots

    def added(slots, count):
        return sum(slots[k] for k in range(count))

    p_part = halves(dot(split(halves(u)), norms[...], 1, 0))
    for f in range(8):
        ps[f] = p_part[:, f * 128 : (f + 1) * 128]
    done = scatter(ps, p0, fs, peer_f, 8)
    gradient(0)
    depart(0)
    gradient(1)
    depart(1)
    p_sum = added(done(), 8) + p_error
    p_sum = added(spread(p1, at_a, peer_a, 8, p_sum)(), 8)
    done = spread(p2, at_b, peer_b, 8, p_sum)
    merge(0)
    gradient(2)
    gradient(3)
    p_sum = added(done(), 8) * (1.0 / REPS)
    done = spread(pn, fs, peer_f, 8, p_sum)
    depart(2)
    done()
    p_all = jnp.concatenate([pn[f] for f in range(8)], axis=1)

    v = halves(dot(split(p_all), norms[...], 1, 1))
    q_hidden = halves(dot(split(v), hidden[...], 1, 0))
    q_error = halves(dot(split(p_sum), err_v[...], 1, 0))
    for at in range(16):
        qs[at] = q_error[:, at * 128 : (at + 1) * 128]
    for at in range(8):
        qs[core * 8 + at] += q_hidden[:, at * 128 : (at + 1) * 128]
    done = scatter(qs, r1, at_c, peer_c, 16)
    merge(1)
    depart(3)

    gram_v[...] = jnp.zeros_like(gram_v)
    gram_v[:, 0:RANK] = dot(p_all, p_all, 1, 1, HIGHEST)
    gram = gram_v[...]
    lane = lax.broadcasted_iota(jnp.int32, (8, 128), 1)
    row = lax.broadcasted_iota(jnp.int32, (8, 128), 0)
    inverse = jnp.where(lane == row, 1.0, 0.0).astype(F32)
    scale = jnp.zeros((8, 1), F32)
    for k in range(RANK):
        column = jnp.sum(jnp.where(lane == k, gram, 0.0), axis=1, keepdims=True)
        pivot = column[k : k + 1, :]
        scale = jnp.where(row[:, 0:1] == k, lax.rsqrt(pivot), scale)
        factor = jnp.where(row[:, 0:1] > k, column / pivot, 0.0)
        gram = gram - factor * gram[k : k + 1, :]
        inverse = inverse - factor * inverse[k : k + 1, :]
    inverse = (inverse * scale)[:, 0:RANK]
    p_orth = dot(inverse, p_sum, 1, 0, HIGHEST)
    high = p_orth.astype(BF16).astype(F32)
    p_cols = jnp.concatenate([high, p_orth - high, high], axis=0).T.astype(BF16)

    collect(0)
    done = spread(q1, at_d, peer_d, 4, added(done(), 16))
    merge(2)
    done = spread(q2, at_b, peer_b, 8, added(done(), 4))
    merge(3)
    collect(1)
    collect(2)
    q_sum = added(done(), 8) * (1.0 / REPS)
    done = spread(qn, at_c, peer_c, 16, dot(inverse, q_sum, 1, 0, HIGHEST))
    collect(3)
    for b in range(BLOCKS):
        arrived(rs.at[b], m[b]["sib"])
        arrived(ry.at[b, 0], m[b]["same"])
        arrived(ry.at[b, 1], m[b]["cross"])
    done()

    for which, first, second in ((core, own, 0), (1 - core, rs, 1)):
        for b in range(BLOCKS):
            for side in range(2):
                at = which * 8 + b * 2 + side
                columns = pl.ds(pl.multiple_of(at * 128, 128), 128)
                part = slice(side * 128, (side + 1) * 128)
                q_piece = qn[at]
                q_v[:, columns] = q_piece
                high = q_piece.astype(BF16).astype(F32)
                q_rows = jnp.concatenate([high, high, q_piece - high], axis=0).astype(BF16)
                approx = dot(p_cols, q_rows, 1, 0)
                value = first[b, :, part].astype(F32) + ry[b, second, :, part].astype(F32)
                value = value + err_v[:, columns].astype(F32)
                eo_v[:, columns] = (value - approx).astype(BF16)
                m_new = 0.9 * m1_v[:, columns].astype(F32) + 0.1 * approx
                v_new = 0.999 * m2_v[:, columns].astype(F32) + 0.001 * approx * approx
                below = jnp.sqrt(v_new * (1.0 / (1.0 - 0.999**10))) + 1e-08
                adam_v[:, columns] = (m_new * (1.0 / (1.0 - 0.9**10)) / below).astype(BF16)

    last = [
        pltpu.make_async_copy(src, dst, lsem.at[at])
        for at, (src, dst) in enumerate(
            [(adam_v, adam_out), (eo_v, error_out.at[0]), (q_v, q_out)]
        )
    ]
    for copy in last:
        copy.start()
    for copy in pending:
        copy.wait_send()

    @pl.when(native)
    def _():
        for copy in own_sends:
            copy.wait_send()

    @pl.when(jnp.logical_not(native))
    def _():
        for copy in base_sends:
            copy.wait_send()

    for copy in last:
        copy.wait()


def _fsdp_peers(dev, fs, step, core):
    f = lax.rem(fs + step, 8)
    return [dev(y_hi=f // 4, x=lax.rem(f, 4), core=c) for c in (core, 1 - core)]


def shards(frames, cotangent, norm_gain, w_in, w_out, error_in, q_start, moment_one, moment_two):
    any_space = pl.BlockSpec(memory_space=pl.ANY)
    vmem = pltpu.VMEM
    adam, error, q_new = pl.pallas_call(
        kernel,
        out_shape=(
            jax.ShapeDtypeStruct((128, FFW), BF16),
            jax.ShapeDtypeStruct((1, 128, FFW), BF16),
            jax.ShapeDtypeStruct((RANK, FFW), F32),
        ),
        in_specs=[any_space] * 9,
        out_specs=(any_space,) * 3,
        scratch_shapes=[
            vmem((TOK, D), BF16),
            vmem((1, D), F32),
            vmem((2 * TOK, D), BF16),
            vmem((2 * TOK, D), BF16),
            vmem((2, D, TOK), BF16),
            vmem((D, HALF), BF16),
            vmem((HALF, D), BF16),
            vmem((2 * TOK, HALF), F32),
            vmem((2 * TOK, HALF), BF16),
            vmem((BLOCKS, 4, 2, 256, BLK), BF16),
            vmem((BLOCKS, 2, 256, BLK), BF16),
            vmem((BLOCKS, 2, 256, BLK), BF16),
            vmem((BLOCKS, 2, 256, BLK), BF16),
            vmem((BLOCKS, 2, 256, BLK), BF16),
            vmem((BLOCKS, 2, 128, BLK), BF16),
            vmem((BLOCKS, 128, BLK), BF16),
            vmem((BLOCKS, 2, 128, BLK), BF16),
            vmem((BLOCKS, 128, BLK), BF16),
            vmem((BLOCKS, 128, BLK), F32),
            vmem((128, FFW), BF16),
            vmem((128, FFW), BF16),
            vmem((128, FFW), BF16),
            vmem((RANK, FFW), F32),
            vmem((16, FFW), BF16),
            vmem((8, RANK, 128), F32),
            vmem((8, RANK, 128), F32),
            vmem((8, RANK, 128), F32),
            vmem((8, RANK, 128), F32),
            vmem((8, RANK, 128), F32),
            vmem((16, RANK, 128), F32),
            vmem((16, RANK, 128), F32),
            vmem((4, RANK, 128), F32),
            vmem((8, RANK, 128), F32),
            vmem((16, RANK, 128), F32),
            vmem((128, FFW), BF16),
            vmem((128, FFW), BF16),
            vmem((RANK, 128), F32),
            pltpu.SemaphoreType.REGULAR((2,)),
            pltpu.SemaphoreType.DMA((16,)),
            pltpu.SemaphoreType.DMA((SEMS,)),
            pltpu.SemaphoreType.DMA((SEMS,)),
        ],
        compiler_params=pltpu.CompilerParams(
            collective_id=0, has_side_effects=True, vmem_limit_bytes=60 * 1024 * 1024
        ),
        cost_estimate=pl.CostEstimate(
            flops=6 * TOK * D * FFW, bytes_accessed=6 << 20, transcendentals=TOK * FFW
        ),
    )(
        frames, cotangent, norm_gain.reshape(1, D), w_in, w_out, error_in, q_start.T,
        moment_one, moment_two,
    )
    return adam, error, q_new.T


def solution(mesh):
    return jax.shard_map(
        shards,
        mesh=mesh,
        in_specs=(
            P("rep", "fsdp", None),
            P("rep", "fsdp", None),
            P(),
            P("fsdp", None),
            P("fsdp", None),
            P("rep", "fsdp", None),
            P(),
            P("fsdp", None),
            P("fsdp", None),
        ),
        out_specs=(P("fsdp", None), P("rep", "fsdp", None), P()),
        check_vma=False,
    )
```

```python
import functools

import jax
import jax.numpy as jnp
from jax import lax
from jax.experimental import pallas as pl
from jax.experimental.pallas import tpu as pltpu
from jax.sharding import PartitionSpec as P

MESH = pl.DeviceIdType.MESH
HIGHEST = lax.Precision.HIGHEST
F32, BF16 = jnp.float32, jnp.bfloat16

D, FFW, RANK, TOK = 1024, 2048, 8, 320
HALF = FFW // 2
BLK, BLOCKS = 256, 4
REPS = 64
SEMS = 160


def dot(left, right, left_dim, right_dim, precision=None):
    return lax.dot_general(
        left,
        right,
        (((left_dim,), (right_dim,)), ((), ())),
        precision=precision,
        preferred_element_type=F32,
    )


def split(value):
    high = value.astype(BF16).astype(F32)
    return jnp.concatenate([high, value - high], axis=0).astype(BF16)


def halves(rows):
    return rows[0:8, :] + rows[8:16, :]


def kernel(
    frames, cot, gain, w_in, w_out, error, q_start,
    tot_out, approx_out, q_out,
    x_buf, gain_v, norms, cots, norm_t, wi, wo, slope, hidden, g, ra, rb, rc, mc, ty, sb, ry, rs, own,
    yr, g2,
    err_v, q_v, q16, ps, p0, p1, p2, pn, qs, r1, q1, q2, qn, tot, approx_v, gram_v,
    known, lsem, ssem, rsem,
):
    rep, fs = lax.axis_index("rep"), lax.axis_index("fsdp")
    core, z, y_lo = lax.rem(rep, 2), lax.rem(rep // 2, 16), rep // 32
    x, y_hi = lax.rem(fs, 4), fs // 4

    def dev(y_lo=y_lo, z=z, core=core, y_hi=y_hi, x=x):
        return ((y_lo * 16 + z) * 2 + core, y_hi * 4 + x)

    x_next, x_prev, x_far = lax.rem(x + 1, 4), lax.rem(x + 3, 4), lax.rem(x + 2, 4)
    right, left = dev(x=x_next), dev(x=x_prev)
    across = dev(y_lo=1 - y_lo, y_hi=1 - y_hi)
    sibling = dev(core=1 - core)
    beside, above, below = dev(y_lo=1 - y_lo), dev(z=lax.rem(z + 1, 16)), dev(z=lax.rem(z + 15, 16))
    native = core == y_hi

    at_a = (y_lo * 2 + lax.rem(z, 2)) * 2 + core

    def peer_a(k):
        m = lax.rem(at_a + k, 8)
        return m, dev(y_lo=m // 4, z=(z // 2) * 2 + lax.rem(m // 2, 2), core=lax.rem(m, 2))

    at_b = z // 2

    def peer_b(k):
        m = lax.rem(at_b + k, 8)
        return m, dev(z=m * 2 + lax.rem(z, 2))

    at_c = fs * 2 + core

    def peer_c(k):
        m = lax.rem(at_c + k, 16)
        f = m // 2
        return m, dev(y_hi=f // 4, x=lax.rem(f, 4), core=lax.rem(m, 2))

    def peer_f(k):
        f = lax.rem(fs + k, 8)
        return f, dev(y_hi=f // 4, x=lax.rem(f, 4))

    at_d = y_lo * 2 + lax.rem(z, 2)

    def peer_d(k):
        m = lax.rem(at_d + k, 4)
        return m, dev(y_lo=m // 2, z=(z // 2) * 2 + lax.rem(m, 2))

    ids = iter(range(SEMS))
    pending = []

    def remote(src, dst, at, device):
        return pltpu.make_async_remote_copy(
            src_ref=src, dst_ref=dst, send_sem=ssem.at[at], recv_sem=rsem.at[at],
            device_id=device, device_id_type=MESH,
        )

    def send(src, dst, at, device):
        copy = remote(src, dst, at, device)
        copy.start()
        pending.append(copy)

    def arrived(dst, at):
        remote(dst, dst, at, sibling).wait_recv()

    def in_rows(shard, kind, start=0, count=64):
        return wi.at[pl.ds(pl.multiple_of(shard * 128 + kind * 64 + start, 32), count)]

    def out_rows(shard, kind, start=0, count=128):
        return wo.at[pl.ds(pl.multiple_of(shard * 256 + kind * 128 + start, 64), count)]

    def tokens(which):
        return pl.ds(pl.multiple_of(which * TOK, TOK), TOK)

    half = w_in.at[:, pl.ds(pl.multiple_of(core * HALF, HALF), HALF)]
    mine = lax.rem(z + y_lo, 2)
    rest = 1 - mine

    def own_in(kind):
        return half.at[pl.ds(pl.multiple_of(kind * 64, 64), 64)]

    def own_out(kind):
        return w_out.at[pl.ds(pl.multiple_of(kind * 128, 128), 128)]

    local = [
        pltpu.make_async_copy(src, dst, lsem.at[at])
        for at, (src, dst) in enumerate(
            [
                (frames.at[0], x_buf),
                (gain, gain_v),
                (cot.at[0], cots.at[tokens(core)]),
                (half, wi.at[pl.ds(pl.multiple_of(fs * 128, 128), 128)]),
                (error.at[0], err_v),
                (q_start, q_v),
            ]
        )
    ]
    for copy in local:
        copy.start()
    base_out = pltpu.make_async_copy(
        w_out, wo.at[pl.ds(pl.multiple_of(x * 256, 256), 256)], lsem.at[len(local)]
    )

    @pl.when(native)
    def _():
        base_out.start()

    barrier = pltpu.get_barrier_semaphore()
    peers = [peer_a(k)[1] for k in range(1, 8)] + [peer_b(k)[1] for k in (1, 7)]
    peers += [across, dev(z=lax.rem(z + 15 + 2 * lax.rem(z, 2), 16))]
    peers += [one for f in range(1, 8) for one in _fsdp_peers(dev, fs, f, core)]
    for peer in peers:
        pl.semaphore_signal(barrier, inc=1, device_id=peer, device_id_type=MESH)
    pl.semaphore_wait(barrier, len(peers))

    def vouch(level):
        for k in (2**level, 8 - 2**level):
            pl.semaphore_signal(
                known.at[level], inc=1, device_id=peer_b(k)[1], device_id_type=MESH
            )

    vouch(0)

    n = {name: next(ids) for name in (
        "y1", "y2", "a_p", "a_m", "af_p", "af_m", "b_p", "b_m", "bf_p", "bf_m",
        "oy1", "oy2", "o_p", "o_m", "of_p", "of_m",
        "w1", "w2", "w3", "w4", "w5", "w6", "w7", "w8", "v1", "v2", "v3", "v4", "cot", "norm",
    )}
    g_own = 4 - y_hi * 4 + x
    f_left, f_right, f_far = y_hi * 4 + x_prev, y_hi * 4 + x_next, y_hi * 4 + x_far
    g_left, g_right, g_far = [4 - y_hi * 4 + at for at in (x_prev, x_next, x_far)]

    def pass_on(place, name, device):
        send(place, place, n[name], device)

    send(own_in(rest), in_rows(fs, rest), n["y1"], across)
    send(own_in(mine), in_rows(fs, mine), n["a_p"], right)
    send(own_in(mine), in_rows(fs, mine), n["a_m"], left)
    own_sends = [
        remote(own_out(rest), out_rows(x, rest), n["oy1"], across),
        remote(own_out(mine), out_rows(x, mine), n["o_p"], right),
        remote(own_out(mine), out_rows(x, mine), n["o_m"], left),
        remote(own_out(mine), out_rows(x, mine), n["oy2"], across),
    ]

    @pl.when(native)
    def _():
        for copy in own_sends[:3]:
            copy.start()


    send(own_in(mine), in_rows(fs, mine), n["y2"], across)

    @pl.when(native)
    def _():
        own_sends[3].start()

    send(cot.at[0], cots.at[tokens(core)], n["cot"], sibling)

    local[0].wait()
    local[1].wait()

    @pl.loop(0, TOK // 32)
    def _(step):
        rows = pl.ds(pl.multiple_of(step * 32, 32), 32)
        values = x_buf[rows, :].astype(F32)
        centred = values - jnp.mean(values, axis=-1, keepdims=True)
        variance = jnp.mean(centred * centred, axis=-1, keepdims=True)
        result = (centred * lax.rsqrt(variance + 1e-05) * gain_v[...]).astype(BF16)
        norms[pl.ds(pl.multiple_of(core * TOK + step * 32, 32), 32), :] = result

    send(norms.at[tokens(core)], norms.at[tokens(core)], n["norm"], sibling)

    local[5].wait()
    q16[...] = split(q_v[...])

    base = out_rows(x, mine)
    base_sends = [remote(base, base, n["o_p"], right), remote(base, base, n["o_m"], left)]

    arrived(in_rows(g_own, mine), n["y1"])
    pass_on(in_rows(g_own, mine), "b_p", right)
    pass_on(in_rows(g_own, mine), "b_m", left)
    @pl.when(jnp.logical_not(native))
    def _():
        arrived(base, n["oy1"])
        for copy in base_sends:
            copy.start()

    arrived(in_rows(f_left, mine), n["a_p"])
    pass_on(in_rows(f_left, mine, 0, 32), "af_p", right)
    pass_on(in_rows(f_left, mine), "w1", beside)
    arrived(in_rows(f_right, mine), n["a_m"])
    pass_on(in_rows(f_right, mine, 32, 32), "af_m", left)
    pass_on(in_rows(f_right, mine), "w2", below)

    out_sends = [
        remote(place, place, n[name], device)
        for place, name, device in (
            (out_rows(x_prev, mine, 0, 64), "of_p", right),
            (out_rows(x_prev, mine), "v1", beside),
            (out_rows(x_next, mine, 64, 64), "of_m", left),
            (out_rows(x_next, mine), "v2", below),
        )
    ]

    def pass_out():
        arrived(out_rows(x_prev, mine), n["o_p"])
        out_sends[0].start()
        out_sends[1].start()
        arrived(out_rows(x_next, mine), n["o_m"])
        out_sends[2].start()
        out_sends[3].start()

    @pl.when(native)
    def _():
        pass_out()

    pending.extend(out_sends)
    arrived(in_rows(g_left, mine), n["b_p"])
    pass_on(in_rows(g_left, mine, 0, 32), "bf_p", right)
    pass_on(in_rows(g_left, mine), "w3", above)
    arrived(in_rows(g_right, mine), n["b_m"])
    pass_on(in_rows(g_right, mine, 32, 32), "bf_m", left)
    pass_on(in_rows(g_right, mine), "w4", above)

    @pl.when(jnp.logical_not(native))
    def _():
        pass_out()

    pl.semaphore_wait(known.at[0], 2)
    vouch(1)
    for at, (name, passed, device) in enumerate((("af_p", "w5", below), ("af_m", "w6", below))):
        arrived(in_rows(f_far, mine, at * 32, 32), n[name])
        pass_on(in_rows(f_far, mine, at * 32, 32), passed, device)
    for at, (name, passed) in enumerate((("bf_p", "w7"), ("bf_m", "w8"))):
        arrived(in_rows(g_far, mine, at * 32, 32), n[name])
        pass_on(in_rows(g_far, mine, at * 32, 32), passed, beside)
    for at, (name, passed, device) in enumerate((("of_p", "v3", above), ("of_m", "v4", across))):
        arrived(out_rows(x_far, mine, at * 64, 64), n[name])
        pass_on(out_rows(x_far, mine, at * 64, 64), passed, device)

    norm_t[core] = norms[tokens(core), :].T
    arrived(norms.at[tokens(1 - core)], n["norm"])
    norm_t[1 - core] = norms[tokens(1 - core), :].T
    arrived(cots.at[tokens(1 - core)], n["cot"])
    pl.semaphore_wait(known.at[1], 2)
    for copy in local[2:5] + local[6:]:
        copy.wait()
    arrived(in_rows(g_own, rest), n["y2"])
    for shard, name in ((f_left, "w1"), (f_right, "w2"), (g_left, "w3"), (g_right, "w4")):
        arrived(in_rows(shard, rest), n[name])
    for shard, names in ((f_far, ("w5", "w6")), (g_far, ("w7", "w8"))):
        arrived(in_rows(shard, rest, 0, 32), n[names[0]])
        arrived(in_rows(shard, rest, 32, 32), n[names[1]])

    for b in range(BLOCKS):
        for j in range(2):
            rows, columns = pl.ds(j * TOK, TOK), pl.ds(b * BLK, BLK)
            pre = dot(norms[rows, :], wi[:, columns], 1, 0)
            sig = 1.0 / (1.0 + jnp.exp(-pre))
            slope[rows, columns] = sig * (1.0 + pre * (1.0 - sig))
    p_error = halves(dot(q16[...], err_v[...], 1, 1))

    u = jnp.zeros((16, 2 * TOK), F32)

    def hidden_part(shard, total):
        rows = pl.ds(pl.multiple_of(shard * BLK, BLK), BLK)
        act = dot(cots[...], wo[rows, :], 1, 1)
        value = (act * slope[:, rows]).astype(BF16)
        hidden[:, rows] = value
        q_columns = pl.ds(pl.multiple_of(core * HALF + shard * BLK, BLK), BLK)
        return total + dot(q16[:, q_columns], value, 1, 1)

    @pl.when(native)
    def _():
        base_out.wait()

    @pl.when(jnp.logical_not(native))
    def _():
        arrived(out_rows(x, rest), n["oy2"])

    u = hidden_part(x, u)
    arrived(out_rows(x_prev, rest), n["v1"])
    u = hidden_part(x_prev, u)
    arrived(out_rows(x_next, rest), n["v2"])
    u = hidden_part(x_next, u)
    arrived(out_rows(x_far, rest, 0, 64), n["v3"])
    arrived(out_rows(x_far, rest, 64, 64), n["v4"])
    u = hidden_part(x_far, u)

    kinds = ("a_p", "a_m", "b_p", "b_m", "c_p", "c_m", "same", "cross", "sib")
    m = [{name: next(ids) for name in kinds} for _ in range(BLOCKS)]
    partner_same, partner_cross = dev(y_hi=1 - y_hi), dev(y_hi=1 - y_hi, core=1 - core)
    keep = pl.ds(pl.multiple_of(y_hi * 128, 128), 128)
    give = pl.ds(pl.multiple_of(128 - y_hi * 128, 128), 128)

    def gradient(b):
        for j in range(2):
            piece = hidden[j * TOK : (j + 1) * TOK, b * BLK : (b + 1) * BLK]
            for h in range(2):
                grad = dot(norm_t[j, h * 512 : (h + 1) * 512, :], piece, 1, 0).astype(BF16)
                for to in range(4):
                    g[b, to, j, h * 128 : (h + 1) * 128, :] = grad[to * 128 : (to + 1) * 128]

    def depart(b):
        send(g.at[b, x_far, 0], ra.at[b, 0], m[b]["a_p"], right)
        send(g.at[b, x_far, 1], ra.at[b, 1], m[b]["a_m"], left)
        send(g.at[b, x_next, 1], rb.at[b, 1], m[b]["b_p"], right)
        send(g.at[b, x_prev, 0], rb.at[b, 0], m[b]["b_m"], left)

    def merge(b):
        arrived(ra.at[b, 0], m[b]["a_p"])
        mc[b, 0] = (g[b, x_next, 0].astype(F32) + ra[b, 0].astype(F32)).astype(BF16)
        send(mc.at[b, 0], rc.at[b, 0], m[b]["c_p"], right)
        arrived(ra.at[b, 1], m[b]["a_m"])
        mc[b, 1] = (g[b, x_prev, 1].astype(F32) + ra[b, 1].astype(F32)).astype(BF16)
        send(mc.at[b, 1], rc.at[b, 1], m[b]["c_m"], left)

    def total(b, j, rows):
        return sum(ref[rows, :].astype(F32) for ref in (g.at[b, x, j], rb.at[b, j], rc.at[b, j]))

    def collect(b):
        arrived(rb.at[b, 1], m[b]["b_p"])
        arrived(rb.at[b, 0], m[b]["b_m"])
        arrived(rc.at[b, 0], m[b]["c_p"])
        arrived(rc.at[b, 1], m[b]["c_m"])
        ty[b, 0] = total(b, core, give).astype(BF16)
        send(ty.at[b, 0], ry.at[b, 0], m[b]["same"], partner_same)
        ty[b, 1] = total(b, 1 - core, give).astype(BF16)
        send(ty.at[b, 1], ry.at[b, 1], m[b]["cross"], partner_cross)
        sb[b] = total(b, 1 - core, keep).astype(BF16)
        send(sb.at[b], rs.at[b], m[b]["sib"], sibling)
        own[b] = total(b, core, keep)

    def cross(b):
        send(g.at[b, :, :, give, :], yr, m[b]["same"], partner_same)

    top = pl.ds(0, 128)

    def fold(b):
        arrived(yr, m[b]["same"])
        for to in range(4):
            for j in range(2):
                g2[to, j] = (g[b, to, j, keep, :].astype(F32) + yr[to, j].astype(F32)).astype(BF16)
        send(g2.at[x_far, 0], ra.at[b, 0, top], m[b]["a_p"], right)
        send(g2.at[x_far, 1], ra.at[b, 1, top], m[b]["a_m"], left)
        send(g2.at[x_next, 1], rb.at[b, 1, top], m[b]["b_p"], right)
        send(g2.at[x_prev, 0], rb.at[b, 0, top], m[b]["b_m"], left)

    def merge_folded(b):
        arrived(ra.at[b, 0, top], m[b]["a_p"])
        mc[b, 0, top] = (g2[x_next, 0].astype(F32) + ra[b, 0, top].astype(F32)).astype(BF16)
        send(mc.at[b, 0, top], rc.at[b, 0, top], m[b]["c_p"], right)
        arrived(ra.at[b, 1, top], m[b]["a_m"])
        mc[b, 1, top] = (g2[x_prev, 1].astype(F32) + ra[b, 1, top].astype(F32)).astype(BF16)
        send(mc.at[b, 1, top], rc.at[b, 1, top], m[b]["c_m"], left)

    def total_folded(b, j):
        return sum(part[...].astype(F32) for part in (g2.at[x, j], rb.at[b, j, top], rc.at[b, j, top]))

    def collect_folded(b):
        arrived(rb.at[b, 1, top], m[b]["b_p"])
        arrived(rb.at[b, 0, top], m[b]["b_m"])
        arrived(rc.at[b, 0, top], m[b]["c_p"])
        arrived(rc.at[b, 1, top], m[b]["c_m"])
        sb[b] = total_folded(b, 1 - core).astype(BF16)
        send(sb.at[b], rs.at[b], m[b]["sib"], sibling)
        own[b] = total_folded(b, core)

    def scatter(pieces, slots, at, peer, count):
        names = [next(ids) for _ in range(count - 1)]
        for k in range(1, count):
            to, device = peer(k)
            send(pieces.at[to], slots.at[at], names[k - 1], device)
        slots[at] = pieces[at]
        return functools.partial(landed, slots, peer, count, names)

    def spread(slots, at, peer, count, value):
        slots[at] = value
        names = [next(ids) for _ in range(count - 1)]
        for k in range(1, count):
            send(slots.at[at], slots.at[at], names[k - 1], peer(k)[1])
        return functools.partial(landed, slots, peer, count, names)

    def landed(slots, peer, count, names):
        for k in range(1, count):
            arrived(slots.at[peer(count - k)[0]], names[k - 1])
        return slots

    def added(slots, count):
        return sum(slots[k] for k in range(count))

    p_part = halves(dot(split(halves(u)), norms[...], 1, 0))
    for f in range(8):
        ps[f] = p_part[:, f * 128 : (f + 1) * 128]
    done = scatter(ps, p0, fs, peer_f, 8)
    gradient(0)
    depart(0)
    gradient(2)
    depart(2)
    p_sum = added(done(), 8) + p_error
    done = spread(p1, at_a, peer_a, 8, p_sum)
    gradient(1)
    p_sum = added(done(), 8)
    done = spread(p2, at_b, peer_b, 8, p_sum)
    cross(1)
    merge(0)
    gradient(3)
    p_sum = added(done(), 8) * (1.0 / REPS)
    done = spread(pn, fs, peer_f, 8, p_sum)
    depart(3)
    q_error = halves(dot(split(p_sum), err_v[...], 1, 0))
    for at in range(16):
        qs[at] = q_error[:, at * 128 : (at + 1) * 128]
    done()
    p_all = jnp.concatenate([pn[f] for f in range(8)], axis=1)

    v = halves(dot(split(p_all), norms[...], 1, 1))
    q_hidden = halves(dot(split(v), hidden[...], 1, 0))
    for at in range(8):
        qs[core * 8 + at] += q_hidden[:, at * 128 : (at + 1) * 128]
    done = scatter(qs, r1, at_c, peer_c, 16)
    merge(2)
    fold(1)

    collect(0)
    done = spread(q1, at_d, peer_d, 4, added(done(), 16))
    merge(3)
    done = spread(q2, at_b, peer_b, 8, added(done(), 4))
    merge_folded(1)
    collect(2)

    gram_v[...] = jnp.zeros_like(gram_v)
    gram_v[:, 0:RANK] = dot(p_all, p_all, 1, 1, HIGHEST)
    gram = gram_v[...]
    lane = lax.broadcasted_iota(jnp.int32, (8, 128), 1)
    row = lax.broadcasted_iota(jnp.int32, (8, 128), 0)
    inverse = jnp.where(lane == row, 1.0, 0.0).astype(F32)
    scale = jnp.zeros((8, 1), F32)
    for k in range(RANK):
        column = jnp.sum(jnp.where(lane == k, gram, 0.0), axis=1, keepdims=True)
        pivot = column[k : k + 1, :]
        scale = jnp.where(row[:, 0:1] == k, lax.rsqrt(pivot), scale)
        factor = jnp.where(row[:, 0:1] > k, column / pivot, 0.0)
        gram = gram - factor * gram[k : k + 1, :]
        inverse = inverse - factor * inverse[k : k + 1, :]
    inverse = (inverse * scale)[:, 0:RANK]
    p_orth = dot(inverse, p_sum, 1, 0, HIGHEST)
    high = p_orth.astype(BF16).astype(F32)
    p_cols = jnp.concatenate([high, p_orth - high, high], axis=0).T.astype(BF16)

    collect(3)
    collect_folded(1)
    q_sum = added(done(), 8) * (1.0 / REPS)
    done = spread(qn, at_c, peer_c, 16, dot(inverse, q_sum, 1, 0, HIGHEST))
    for b in range(BLOCKS):
        arrived(rs.at[b], m[b]["sib"])
        if b != 1:
            arrived(ry.at[b, 0], m[b]["same"])
            arrived(ry.at[b, 1], m[b]["cross"])
        for which, first, second in ((core, own, 0), (1 - core, rs, 1)):
            columns = pl.ds(pl.multiple_of(which * HALF + b * BLK, BLK), BLK)
            value = first[b].astype(F32)
            if b != 1:
                value = value + ry[b, second].astype(F32)
            tot[:, columns] = value + err_v[:, columns].astype(F32)
    last = [pltpu.make_async_copy(tot, tot_out, lsem.at[0])]
    last[0].start()
    done()

    for at in range(16):
        columns = pl.ds(at * 128, 128)
        q_piece = qn[at]
        q_v[:, columns] = q_piece
        high = q_piece.astype(BF16).astype(F32)
        q_rows = jnp.concatenate([high, high, q_piece - high], axis=0).astype(BF16)
        approx_v[:, columns] = dot(p_cols, q_rows, 1, 0)

    last.append(pltpu.make_async_copy(approx_v, approx_out, lsem.at[1]))
    last.append(pltpu.make_async_copy(q_v, q_out, lsem.at[2]))
    for copy in last[1:]:
        copy.start()
    for copy in pending:
        copy.wait_send()

    @pl.when(native)
    def _():
        for copy in own_sends:
            copy.wait_send()

    @pl.when(jnp.logical_not(native))
    def _():
        for copy in base_sends:
            copy.wait_send()

    for copy in last:
        copy.wait()


def _fsdp_peers(dev, fs, step, core):
    f = lax.rem(fs + step, 8)
    return [dev(y_hi=f // 4, x=lax.rem(f, 4), core=c) for c in (core, 1 - core)]


def shards(frames, cotangent, norm_gain, w_in, w_out, error_in, q_start, moment_one, moment_two):
    any_space = pl.BlockSpec(memory_space=pl.ANY)
    vmem = pltpu.VMEM
    total, approx, q_new = pl.pallas_call(
        kernel,
        out_shape=(
            jax.ShapeDtypeStruct((128, FFW), F32),
            jax.ShapeDtypeStruct((128, FFW), F32),
            jax.ShapeDtypeStruct((RANK, FFW), F32),
        ),
        in_specs=[any_space] * 7,
        out_specs=(any_space,) * 3,
        scratch_shapes=[
            vmem((TOK, D), BF16),
            vmem((1, D), F32),
            vmem((2 * TOK, D), BF16),
            vmem((2 * TOK, D), BF16),
            vmem((2, D, TOK), BF16),
            vmem((D, HALF), BF16),
            vmem((HALF, D), BF16),
            vmem((2 * TOK, HALF), F32),
            vmem((2 * TOK, HALF), BF16),
            vmem((BLOCKS, 4, 2, 256, BLK), BF16),
            vmem((BLOCKS, 2, 256, BLK), BF16),
            vmem((BLOCKS, 2, 256, BLK), BF16),
            vmem((BLOCKS, 2, 256, BLK), BF16),
            vmem((BLOCKS, 2, 256, BLK), BF16),
            vmem((BLOCKS, 2, 128, BLK), BF16),
            vmem((BLOCKS, 128, BLK), BF16),
            vmem((BLOCKS, 2, 128, BLK), BF16),
            vmem((BLOCKS, 128, BLK), BF16),
            vmem((BLOCKS, 128, BLK), F32),
            vmem((4, 2, 128, BLK), BF16),
            vmem((4, 2, 128, BLK), BF16),
            vmem((128, FFW), BF16),
            vmem((RANK, FFW), F32),
            vmem((16, FFW), BF16),
            vmem((8, RANK, 128), F32),
            vmem((8, RANK, 128), F32),
            vmem((8, RANK, 128), F32),
            vmem((8, RANK, 128), F32),
            vmem((8, RANK, 128), F32),
            vmem((16, RANK, 128), F32),
            vmem((16, RANK, 128), F32),
            vmem((4, RANK, 128), F32),
            vmem((8, RANK, 128), F32),
            vmem((16, RANK, 128), F32),
            vmem((128, FFW), F32),
            vmem((128, FFW), F32),
            vmem((RANK, 128), F32),
            pltpu.SemaphoreType.REGULAR((2,)),
            pltpu.SemaphoreType.DMA((16,)),
            pltpu.SemaphoreType.DMA((SEMS,)),
            pltpu.SemaphoreType.DMA((SEMS,)),
        ],
        compiler_params=pltpu.CompilerParams(
            collective_id=0, has_side_effects=True, vmem_limit_bytes=60 * 1024 * 1024
        ),
        cost_estimate=pl.CostEstimate(
            flops=6 * TOK * D * FFW, bytes_accessed=6 << 20, transcendentals=TOK * FFW
        ),
    )(
        frames, cotangent, norm_gain.reshape(1, D), w_in, w_out, error_in, q_start.T,
    )
    error = (total - approx).astype(BF16)[None]
    m_new = 0.9 * moment_one.astype(F32) + 0.1 * approx
    v_new = 0.999 * moment_two.astype(F32) + 0.001 * approx * approx
    adam = m_new / (1.0 - 0.9**10) / (jnp.sqrt(v_new / (1.0 - 0.999**10)) + 1e-08)
    return adam.astype(BF16), error, q_new.T


def solution(mesh):
    return jax.shard_map(
        shards,
        mesh=mesh,
        in_specs=(
            P("rep", "fsdp", None),
            P("rep", "fsdp", None),
            P(),
            P("fsdp", None),
            P("fsdp", None),
            P("rep", "fsdp", None),
            P(),
            P("fsdp", None),
            P("fsdp", None),
        ),
        out_specs=(P("fsdp", None), P("rep", "fsdp", None), P()),
        check_vma=False,
    )
```

```python
import functools

import jax
import jax.numpy as jnp
from jax import lax
from jax.experimental import pallas as pl
from jax.experimental.pallas import tpu as pltpu
from jax.sharding import PartitionSpec as P

MESH = pl.DeviceIdType.MESH
HIGHEST = lax.Precision.HIGHEST
F32, BF16 = jnp.float32, jnp.bfloat16

D, FFW, RANK, TOK = 1024, 2048, 8, 320
HALF = FFW // 2
BLK, BLOCKS = 256, 4
REPS = 64
SEMS = 160


def dot(left, right, left_dim, right_dim, precision=None):
    return lax.dot_general(
        left,
        right,
        (((left_dim,), (right_dim,)), ((), ())),
        precision=precision,
        preferred_element_type=F32,
    )


def split(value):
    high = value.astype(BF16).astype(F32)
    return jnp.concatenate([high, value - high], axis=0).astype(BF16)


def halves(rows):
    return rows[0:8, :] + rows[8:16, :]


def kernel(
    frames, cot, gain, w_in, w_out, error, q_start, m_one, m_two,
    adam_out, error_out, q_out,
    x_buf, gain_v, norms, cots, norm_t, wi, wo, slope, hidden, g, ra, rb, rc, mc, ty, sb, ry, rs, own,
    err_v, m1_v, m2_v, q_v, q16, ps, p0, p1, p2, pn, qs, r1, q1, q2, qn, adam_v, eo_v, gram_v,
    known, lsem, ssem, rsem,
):
    rep, fs = lax.axis_index("rep"), lax.axis_index("fsdp")
    core, z, y_lo = lax.rem(rep, 2), lax.rem(rep // 2, 16), rep // 32
    x, y_hi = lax.rem(fs, 4), fs // 4

    def dev(y_lo=y_lo, z=z, core=core, y_hi=y_hi, x=x):
        return ((y_lo * 16 + z) * 2 + core, y_hi * 4 + x)

    x_next, x_prev, x_far = lax.rem(x + 1, 4), lax.rem(x + 3, 4), lax.rem(x + 2, 4)
    right, left = dev(x=x_next), dev(x=x_prev)
    across = dev(y_lo=1 - y_lo, y_hi=1 - y_hi)
    sibling = dev(core=1 - core)
    beside, above, below = dev(y_lo=1 - y_lo), dev(z=lax.rem(z + 1, 16)), dev(z=lax.rem(z + 15, 16))
    native = core == y_hi

    at_a = (y_lo * 2 + lax.rem(z, 2)) * 2 + core

    def peer_a(k):
        m = lax.rem(at_a + k, 8)
        return m, dev(y_lo=m // 4, z=(z // 2) * 2 + lax.rem(m // 2, 2), core=lax.rem(m, 2))

    at_b = z // 2

    def peer_b(k):
        m = lax.rem(at_b + k, 8)
        return m, dev(z=m * 2 + lax.rem(z, 2))

    at_c = fs * 2 + core

    def peer_c(k):
        m = lax.rem(at_c + k, 16)
        f = m // 2
        return m, dev(y_hi=f // 4, x=lax.rem(f, 4), core=lax.rem(m, 2))

    def peer_f(k):
        f = lax.rem(fs + k, 8)
        return f, dev(y_hi=f // 4, x=lax.rem(f, 4))

    at_d = y_lo * 2 + lax.rem(z, 2)

    def peer_d(k):
        m = lax.rem(at_d + k, 4)
        return m, dev(y_lo=m // 2, z=(z // 2) * 2 + lax.rem(m, 2))

    ids = iter(range(SEMS))
    pending = []

    def remote(src, dst, at, device):
        return pltpu.make_async_remote_copy(
            src_ref=src, dst_ref=dst, send_sem=ssem.at[at], recv_sem=rsem.at[at],
            device_id=device, device_id_type=MESH,
        )

    def send(src, dst, at, device):
        copy = remote(src, dst, at, device)
        copy.start()
        pending.append(copy)

    def arrived(dst, at):
        remote(dst, dst, at, sibling).wait_recv()

    def in_rows(shard, kind, start=0, count=64):
        return wi.at[pl.ds(pl.multiple_of(shard * 128 + kind * 64 + start, 32), count)]

    def out_rows(shard, kind, start=0, count=128):
        return wo.at[pl.ds(pl.multiple_of(shard * 256 + kind * 128 + start, 64), count)]

    def tokens(which):
        return pl.ds(pl.multiple_of(which * TOK, TOK), TOK)

    half = w_in.at[:, pl.ds(pl.multiple_of(core * HALF, HALF), HALF)]
    mine = lax.rem(z + y_lo, 2)
    rest = 1 - mine

    def own_in(kind):
        return half.at[pl.ds(pl.multiple_of(kind * 64, 64), 64)]

    def own_out(kind):
        return w_out.at[pl.ds(pl.multiple_of(kind * 128, 128), 128)]

    local = [
        pltpu.make_async_copy(src, dst, lsem.at[at])
        for at, (src, dst) in enumerate(
            [
                (frames.at[0], x_buf),
                (gain, gain_v),
                (cot.at[0], cots.at[tokens(core)]),
                (half, wi.at[pl.ds(pl.multiple_of(fs * 128, 128), 128)]),
                (error.at[0], err_v),
                (q_start, q_v),
                (m_one, m1_v),
                (m_two, m2_v),
            ]
        )
    ]
    for copy in local:
        copy.start()
    base_out = pltpu.make_async_copy(
        w_out, wo.at[pl.ds(pl.multiple_of(x * 256, 256), 256)], lsem.at[len(local)]
    )

    @pl.when(native)
    def _():
        base_out.start()

    barrier = pltpu.get_barrier_semaphore()
    peers = [peer_a(k)[1] for k in range(1, 8)] + [peer_b(k)[1] for k in (1, 7)]
    peers += [across, dev(z=lax.rem(z + 15 + 2 * lax.rem(z, 2), 16))]
    peers += [one for f in range(1, 8) for one in _fsdp_peers(dev, fs, f, core)]
    for peer in peers:
        pl.semaphore_signal(barrier, inc=1, device_id=peer, device_id_type=MESH)
    pl.semaphore_wait(barrier, len(peers))

    def vouch(level):
        for k in (2**level, 8 - 2**level):
            pl.semaphore_signal(
                known.at[level], inc=1, device_id=peer_b(k)[1], device_id_type=MESH
            )

    vouch(0)

    n = {name: next(ids) for name in (
        "y1", "y2", "a_p", "a_m", "af_p", "af_m", "b_p", "b_m", "bf_p", "bf_m",
        "oy1", "oy2", "o_p", "o_m", "of_p", "of_m",
        "w1", "w2", "w3", "w4", "w5", "w6", "w7", "w8", "v1", "v2", "v3", "v4", "cot", "norm",
    )}
    g_own = 4 - y_hi * 4 + x
    f_left, f_right, f_far = y_hi * 4 + x_prev, y_hi * 4 + x_next, y_hi * 4 + x_far
    g_left, g_right, g_far = [4 - y_hi * 4 + at for at in (x_prev, x_next, x_far)]

    def pass_on(place, name, device):
        send(place, place, n[name], device)

    send(own_in(rest), in_rows(fs, rest), n["y1"], across)
    send(own_in(mine), in_rows(fs, mine), n["a_p"], right)
    send(own_in(mine), in_rows(fs, mine), n["a_m"], left)
    own_sends = [
        remote(own_out(rest), out_rows(x, rest), n["oy1"], across),
        remote(own_out(mine), out_rows(x, mine), n["o_p"], right),
        remote(own_out(mine), out_rows(x, mine), n["o_m"], left),
        remote(own_out(mine), out_rows(x, mine), n["oy2"], across),
    ]

    @pl.when(native)
    def _():
        for copy in own_sends[:3]:
            copy.start()

    send(own_in(mine), in_rows(fs, mine), n["y2"], across)

    @pl.when(native)
    def _():
        own_sends[3].start()

    send(cot.at[0], cots.at[tokens(core)], n["cot"], sibling)

    local[0].wait()
    local[1].wait()

    @pl.loop(0, TOK // 32)
    def _(step):
        rows = pl.ds(pl.multiple_of(step * 32, 32), 32)
        values = x_buf[rows, :].astype(F32)
        centred = values - jnp.mean(values, axis=-1, keepdims=True)
        variance = jnp.mean(centred * centred, axis=-1, keepdims=True)
        result = (centred * lax.rsqrt(variance + 1e-05) * gain_v[...]).astype(BF16)
        norms[pl.ds(pl.multiple_of(core * TOK + step * 32, 32), 32), :] = result

    send(norms.at[tokens(core)], norms.at[tokens(core)], n["norm"], sibling)

    local[5].wait()
    q16[...] = split(q_v[...])

    arrived(in_rows(g_own, mine), n["y1"])
    pass_on(in_rows(g_own, mine), "b_p", right)
    pass_on(in_rows(g_own, mine), "b_m", left)
    base = out_rows(x, mine)
    base_sends = [remote(base, base, n["o_p"], right), remote(base, base, n["o_m"], left)]

    @pl.when(jnp.logical_not(native))
    def _():
        arrived(base, n["oy1"])
        for copy in base_sends:
            copy.start()

    arrived(in_rows(f_left, mine), n["a_p"])
    pass_on(in_rows(f_left, mine, 0, 32), "af_p", right)
    pass_on(in_rows(f_left, mine), "w1", beside)
    arrived(in_rows(f_right, mine), n["a_m"])
    pass_on(in_rows(f_right, mine, 32, 32), "af_m", left)
    pass_on(in_rows(f_right, mine), "w2", below)

    out_sends = [
        remote(place, place, n[name], device)
        for place, name, device in (
            (out_rows(x_prev, mine, 0, 64), "of_p", right),
            (out_rows(x_prev, mine), "v1", beside),
            (out_rows(x_next, mine, 64, 64), "of_m", left),
            (out_rows(x_next, mine), "v2", below),
        )
    ]

    def pass_out():
        arrived(out_rows(x_prev, mine), n["o_p"])
        out_sends[0].start()
        out_sends[1].start()
        arrived(out_rows(x_next, mine), n["o_m"])
        out_sends[2].start()
        out_sends[3].start()

    @pl.when(native)
    def _():
        pass_out()

    pending.extend(out_sends)
    arrived(in_rows(g_left, mine), n["b_p"])
    pass_on(in_rows(g_left, mine, 0, 32), "bf_p", right)
    pass_on(in_rows(g_left, mine), "w3", above)
    arrived(in_rows(g_right, mine), n["b_m"])
    pass_on(in_rows(g_right, mine, 32, 32), "bf_m", left)
    pass_on(in_rows(g_right, mine), "w4", above)

    @pl.when(jnp.logical_not(native))
    def _():
        pass_out()

    pl.semaphore_wait(known.at[0], 2)
    vouch(1)
    for at, (name, passed, device) in enumerate((("af_p", "w5", below), ("af_m", "w6", below))):
        arrived(in_rows(f_far, mine, at * 32, 32), n[name])
        pass_on(in_rows(f_far, mine, at * 32, 32), passed, device)
    for at, (name, passed) in enumerate((("bf_p", "w7"), ("bf_m", "w8"))):
        arrived(in_rows(g_far, mine, at * 32, 32), n[name])
        pass_on(in_rows(g_far, mine, at * 32, 32), passed, beside)
    for at, (name, passed, device) in enumerate((("of_p", "v3", above), ("of_m", "v4", across))):
        arrived(out_rows(x_far, mine, at * 64, 64), n[name])
        pass_on(out_rows(x_far, mine, at * 64, 64), passed, device)

    norm_t[core] = norms[tokens(core), :].T
    arrived(norms.at[tokens(1 - core)], n["norm"])
    norm_t[1 - core] = norms[tokens(1 - core), :].T
    arrived(cots.at[tokens(1 - core)], n["cot"])
    pl.semaphore_wait(known.at[1], 2)
    for copy in local[2:5] + local[6:]:
        copy.wait()
    arrived(in_rows(g_own, rest), n["y2"])
    for shard, name in ((f_left, "w1"), (f_right, "w2"), (g_left, "w3"), (g_right, "w4")):
        arrived(in_rows(shard, rest), n[name])
    for shard, names in ((f_far, ("w5", "w6")), (g_far, ("w7", "w8"))):
        arrived(in_rows(shard, rest, 0, 32), n[names[0]])
        arrived(in_rows(shard, rest, 32, 32), n[names[1]])

    for b in range(BLOCKS):
        for j in range(2):
            rows, columns = pl.ds(j * TOK, TOK), pl.ds(b * BLK, BLK)
            pre = dot(norms[rows, :], wi[:, columns], 1, 0)
            sig = 1.0 / (1.0 + jnp.exp(-pre))
            slope[rows, columns] = sig * (1.0 + pre * (1.0 - sig))
    p_error = halves(dot(q16[...], err_v[...], 1, 1))

    @pl.when(native)
    def _():
        base_out.wait()

    @pl.when(jnp.logical_not(native))
    def _():
        arrived(out_rows(x, rest), n["oy2"])

    arrived(out_rows(x_prev, rest), n["v1"])
    arrived(out_rows(x_next, rest), n["v2"])
    arrived(out_rows(x_far, rest, 0, 64), n["v3"])
    arrived(out_rows(x_far, rest, 64, 64), n["v4"])

    u = jnp.zeros((16, 2 * TOK), F32)
    for b in range(BLOCKS):
        columns = pl.ds(b * BLK, BLK)
        act = dot(cots[...], wo[b * BLK : (b + 1) * BLK, :], 1, 1)
        hidden[:, columns] = (act * slope[:, columns]).astype(BF16)
        q_columns = pl.ds(pl.multiple_of(core * HALF + b * BLK, BLK), BLK)
        u += dot(q16[:, q_columns], hidden[:, columns], 1, 1)

    kinds = ("a_p", "a_m", "b_p", "b_m", "c_p", "c_m", "same", "cross", "sib")
    m = [{name: next(ids) for name in kinds} for _ in range(BLOCKS)]
    partner_same, partner_cross = dev(y_hi=1 - y_hi), dev(y_hi=1 - y_hi, core=1 - core)
    keep = pl.ds(pl.multiple_of(y_hi * 128, 128), 128)
    give = pl.ds(pl.multiple_of(128 - y_hi * 128, 128), 128)

    def gradient(b):
        for j in range(2):
            piece = hidden[j * TOK : (j + 1) * TOK, b * BLK : (b + 1) * BLK]
            for h in range(2):
                grad = dot(norm_t[j, h * 512 : (h + 1) * 512, :], piece, 1, 0).astype(BF16)
                for to in range(4):
                    g[b, to, j, h * 128 : (h + 1) * 128, :] = grad[to * 128 : (to + 1) * 128]

    def depart(b):
        send(g.at[b, x_far, 0], ra.at[b, 0], m[b]["a_p"], right)
        send(g.at[b, x_far, 1], ra.at[b, 1], m[b]["a_m"], left)
        send(g.at[b, x_next, 1], rb.at[b, 1], m[b]["b_p"], right)
        send(g.at[b, x_prev, 0], rb.at[b, 0], m[b]["b_m"], left)

    def merge(b):
        arrived(ra.at[b, 0], m[b]["a_p"])
        mc[b, 0] = (g[b, x_next, 0].astype(F32) + ra[b, 0].astype(F32)).astype(BF16)
        send(mc.at[b, 0], rc.at[b, 0], m[b]["c_p"], right)
        arrived(ra.at[b, 1], m[b]["a_m"])
        mc[b, 1] = (g[b, x_prev, 1].astype(F32) + ra[b, 1].astype(F32)).astype(BF16)
        send(mc.at[b, 1], rc.at[b, 1], m[b]["c_m"], left)

    def total(b, j, rows):
        return sum(ref[rows, :].astype(F32) for ref in (g.at[b, x, j], rb.at[b, j], rc.at[b, j]))

    def collect(b):
        arrived(rb.at[b, 1], m[b]["b_p"])
        arrived(rb.at[b, 0], m[b]["b_m"])
        arrived(rc.at[b, 0], m[b]["c_p"])
        arrived(rc.at[b, 1], m[b]["c_m"])
        ty[b, 0] = total(b, core, give).astype(BF16)
        send(ty.at[b, 0], ry.at[b, 0], m[b]["same"], partner_same)
        ty[b, 1] = total(b, 1 - core, give).astype(BF16)
        send(ty.at[b, 1], ry.at[b, 1], m[b]["cross"], partner_cross)
        sb[b] = total(b, 1 - core, keep).astype(BF16)
        send(sb.at[b], rs.at[b], m[b]["sib"], sibling)
        own[b] = total(b, core, keep)

    def scatter(pieces, slots, at, peer, count):
        names = [next(ids) for _ in range(count - 1)]
        for k in range(1, count):
            to, device = peer(k)
            send(pieces.at[to], slots.at[at], names[k - 1], device)
        slots[at] = pieces[at]
        return functools.partial(landed, slots, peer, count, names)

    def spread(slots, at, peer, count, value):
        slots[at] = value
        names = [next(ids) for _ in range(count - 1)]
        for k in range(1, count):
            send(slots.at[at], slots.at[at], names[k - 1], peer(k)[1])
        return functools.partial(landed, slots, peer, count, names)

    def landed(slots, peer, count, names):
        for k in range(1, count):
            arrived(slots.at[peer(count - k)[0]], names[k - 1])
        return slots

    def added(slots, count):
        return sum(slots[k] for k in range(count))

    p_part = halves(dot(split(halves(u)), norms[...], 1, 0))
    for f in range(8):
        ps[f] = p_part[:, f * 128 : (f + 1) * 128]
    done = scatter(ps, p0, fs, peer_f, 8)
    gradient(0)
    depart(0)
    gradient(1)
    depart(1)
    p_sum = added(done(), 8) + p_error
    p_sum = added(spread(p1, at_a, peer_a, 8, p_sum)(), 8)
    done = spread(p2, at_b, peer_b, 8, p_sum)
    merge(0)
    gradient(2)
    gradient(3)
    p_sum = added(done(), 8) * (1.0 / REPS)
    done = spread(pn, fs, peer_f, 8, p_sum)
    depart(2)
    q_error = halves(dot(split(p_sum), err_v[...], 1, 0))
    for at in range(16):
        qs[at] = q_error[:, at * 128 : (at + 1) * 128]
    done()
    p_all = jnp.concatenate([pn[f] for f in range(8)], axis=1)

    v = halves(dot(split(p_all), norms[...], 1, 1))
    q_hidden = halves(dot(split(v), hidden[...], 1, 0))
    for at in range(8):
        qs[core * 8 + at] += q_hidden[:, at * 128 : (at + 1) * 128]
    done = scatter(qs, r1, at_c, peer_c, 16)
    merge(1)
    depart(3)

    collect(0)
    done = spread(q1, at_d, peer_d, 4, added(done(), 16))
    merge(2)
    done = spread(q2, at_b, peer_b, 8, added(done(), 4))
    merge(3)
    collect(1)

    gram_v[...] = jnp.zeros_like(gram_v)
    gram_v[:, 0:RANK] = dot(p_all, p_all, 1, 1, HIGHEST)
    gram = gram_v[...]
    lane = lax.broadcasted_iota(jnp.int32, (8, 128), 1)
    row = lax.broadcasted_iota(jnp.int32, (8, 128), 0)
    inverse = jnp.where(lane == row, 1.0, 0.0).astype(F32)
    scale = jnp.zeros((8, 1), F32)
    for k in range(RANK):
        column = jnp.sum(jnp.where(lane == k, gram, 0.0), axis=1, keepdims=True)
        pivot = column[k : k + 1, :]
        scale = jnp.where(row[:, 0:1] == k, lax.rsqrt(pivot), scale)
        factor = jnp.where(row[:, 0:1] > k, column / pivot, 0.0)
        gram = gram - factor * gram[k : k + 1, :]
        inverse = inverse - factor * inverse[k : k + 1, :]
    inverse = (inverse * scale)[:, 0:RANK]
    p_orth = dot(inverse, p_sum, 1, 0, HIGHEST)
    high = p_orth.astype(BF16).astype(F32)
    p_cols = jnp.concatenate([high, p_orth - high, high], axis=0).T.astype(BF16)

    collect(2)
    q_sum = added(done(), 8) * (1.0 / REPS)
    done = spread(qn, at_c, peer_c, 16, dot(inverse, q_sum, 1, 0, HIGHEST))
    collect(3)
    for b in range(BLOCKS):
        arrived(rs.at[b], m[b]["sib"])
        arrived(ry.at[b, 0], m[b]["same"])
        arrived(ry.at[b, 1], m[b]["cross"])
    done()

    for which, first, second in ((core, own, 0), (1 - core, rs, 1)):
        for b in range(BLOCKS):
            for side in range(2):
                at = which * 8 + b * 2 + side
                columns = pl.ds(pl.multiple_of(at * 128, 128), 128)
                part = slice(side * 128, (side + 1) * 128)
                q_piece = qn[at]
                q_v[:, columns] = q_piece
                high = q_piece.astype(BF16).astype(F32)
                q_rows = jnp.concatenate([high, high, q_piece - high], axis=0).astype(BF16)
                approx = dot(p_cols, q_rows, 1, 0)
                value = first[b, :, part].astype(F32) + ry[b, second, :, part].astype(F32)
                value = value + err_v[:, columns].astype(F32)
                eo_v[:, columns] = (value - approx).astype(BF16)
                m_new = 0.9 * m1_v[:, columns].astype(F32) + 0.1 * approx
                v_new = 0.999 * m2_v[:, columns].astype(F32) + 0.001 * approx * approx
                below = jnp.sqrt(v_new * (1.0 / (1.0 - 0.999**10))) + 1e-08
                adam_v[:, columns] = (m_new * (1.0 / (1.0 - 0.9**10)) / below).astype(BF16)

    last = [
        pltpu.make_async_copy(src, dst, lsem.at[at])
        for at, (src, dst) in enumerate(
            [(adam_v, adam_out), (eo_v, error_out.at[0]), (q_v, q_out)]
        )
    ]
    for copy in last:
        copy.start()
    for copy in pending:
        copy.wait_send()

    @pl.when(native)
    def _():
        for copy in own_sends:
            copy.wait_send()

    @pl.when(jnp.logical_not(native))
    def _():
        for copy in base_sends:
            copy.wait_send()

    for copy in last:
        copy.wait()


def _fsdp_peers(dev, fs, step, core):
    f = lax.rem(fs + step, 8)
    return [dev(y_hi=f // 4, x=lax.rem(f, 4), core=c) for c in (core, 1 - core)]


def shards(frames, cotangent, norm_gain, w_in, w_out, error_in, q_start, moment_one, moment_two):
    any_space = pl.BlockSpec(memory_space=pl.ANY)
    vmem = pltpu.VMEM
    adam, error, q_new = pl.pallas_call(
        kernel,
        out_shape=(
            jax.ShapeDtypeStruct((128, FFW), BF16),
            jax.ShapeDtypeStruct((1, 128, FFW), BF16),
            jax.ShapeDtypeStruct((RANK, FFW), F32),
        ),
        in_specs=[any_space] * 9,
        out_specs=(any_space,) * 3,
        scratch_shapes=[
            vmem((TOK, D), BF16),
            vmem((1, D), F32),
            vmem((2 * TOK, D), BF16),
            vmem((2 * TOK, D), BF16),
            vmem((2, D, TOK), BF16),
            vmem((D, HALF), BF16),
            vmem((HALF, D), BF16),
            vmem((2 * TOK, HALF), F32),
            vmem((2 * TOK, HALF), BF16),
            vmem((BLOCKS, 4, 2, 256, BLK), BF16),
            vmem((BLOCKS, 2, 256, BLK), BF16),
            vmem((BLOCKS, 2, 256, BLK), BF16),
            vmem((BLOCKS, 2, 256, BLK), BF16),
            vmem((BLOCKS, 2, 256, BLK), BF16),
            vmem((BLOCKS, 2, 128, BLK), BF16),
            vmem((BLOCKS, 128, BLK), BF16),
            vmem((BLOCKS, 2, 128, BLK), BF16),
            vmem((BLOCKS, 128, BLK), BF16),
            vmem((BLOCKS, 128, BLK), F32),
            vmem((128, FFW), BF16),
            vmem((128, FFW), BF16),
            vmem((128, FFW), BF16),
            vmem((RANK, FFW), F32),
            vmem((16, FFW), BF16),
            vmem((8, RANK, 128), F32),
            vmem((8, RANK, 128), F32),
            vmem((8, RANK, 128), F32),
            vmem((8, RANK, 128), F32),
            vmem((8, RANK, 128), F32),
            vmem((16, RANK, 128), F32),
            vmem((16, RANK, 128), F32),
            vmem((4, RANK, 128), F32),
            vmem((8, RANK, 128), F32),
            vmem((16, RANK, 128), F32),
            vmem((128, FFW), BF16),
            vmem((128, FFW), BF16),
            vmem((RANK, 128), F32),
            pltpu.SemaphoreType.REGULAR((2,)),
            pltpu.SemaphoreType.DMA((16,)),
            pltpu.SemaphoreType.DMA((SEMS,)),
            pltpu.SemaphoreType.DMA((SEMS,)),
        ],
        compiler_params=pltpu.CompilerParams(
            collective_id=0, has_side_effects=True, vmem_limit_bytes=60 * 1024 * 1024
        ),
        cost_estimate=pl.CostEstimate(
            flops=6 * TOK * D * FFW, bytes_accessed=6 << 20, transcendentals=TOK * FFW
        ),
    )(
        frames, cotangent, norm_gain.reshape(1, D), w_in, w_out, error_in, q_start.T,
        moment_one, moment_two,
    )
    return adam, error, q_new.T


def solution(mesh):
    return jax.shard_map(
        shards,
        mesh=mesh,
        in_specs=(
            P("rep", "fsdp", None),
            P("rep", "fsdp", None),
            P(),
            P("fsdp", None),
            P("fsdp", None),
            P("rep", "fsdp", None),
            P(),
            P("fsdp", None),
            P("fsdp", None),
        ),
        out_specs=(P("fsdp", None), P("rep", "fsdp", None), P()),
        check_vma=False,
    )
```
